128 devices in a mesh: wide: 16 (over z_lo, y, core), narrow: 8 (over x, z_hi).
Axes of the slice: x: 4, y: 4, z: 4 (z_hi: 2, z_lo: 2; z = z_hi * 2 + z_lo), core: 2. Of those that a mesh axis runs over, the one named last changes fastest.
Arguments:
- tokens: bfloat16 [512, 16384], P('wide', 'narrow'), may hold values from -6 to 6
- gate_codes: bfloat16 [16384, 26624], P('narrow', 'wide'), may hold values from -8 to 7, as said below
- up_codes: bfloat16 [16384, 26624], P('narrow', 'wide'), may hold values from -8 to 7, as said below
- gate_scale: float32 [128, 26624], P('narrow', 'wide'), may hold values from 0.0009 to 0.003
- up_scale: float32 [128, 26624], P('narrow', 'wide'), may hold values from 0.0009 to 0.003
- down_codes: bfloat16 [26624, 16384], P('wide', 'narrow'), may hold values from -8 to 7, as said below
- down_scale: float32 [208, 16384], P('wide', 'narrow'), may hold values from 0.0007 to 0.0024
- gate_left: float32 [16384, 128], P('narrow'), may hold values from -0.046875 to 0.046875
- gate_right: float32 [128, 26624], P(None, 'wide'), may hold values from -0.5 to 0.5
- up_left: float32 [16384, 128], P('narrow'), may hold values from -0.046875 to 0.046875
- up_right: float32 [128, 26624], P(None, 'wide'), may hold values from -0.5 to 0.5
- down_left: float32 [26624, 128], P('wide'), may hold values from -0.0390625 to 0.0390625
- down_right: float32 [128, 16384], P(None, 'narrow'), may hold values from -0.5 to 0.5
Outputs:
- mixed: float32 [512, 16384], P('wide', 'narrow')
The draws below stay inside these ranges and needn't reach their ends.
Inputs may be any that keep to these rules, and one draw needn't show every extreme that they name: `gate_codes`: integer values. `up_codes`: integer values. `down_codes`: integer values.
All inputs are finite; a program needn't handle non-finite values.
Results may differ from the reference program's by a relative error of at most 0.011.
Values may be sent and summed in bfloat16 or wider, within the bound.
A program may use at most 128 MiB of HBM per device.

```python
import math
import jax
import jax.numpy as jnp
from jax import lax

D = 16384
FF = 26624
RANK = 128
GROUP = 128
TOKENS = 512
N_WIDE = 16


def code_table(key, rows, cols):
    return jax.random.randint(key, (rows, cols), 0, 16).astype(jnp.float32) - 8.0


def draw_gate_codes(key, part):
    key = jax.random.fold_in(key, 11)
    return code_table(key, D, FF).astype(jnp.bfloat16)


def draw_up_codes(key, part):
    key = jax.random.fold_in(key, 12)
    return code_table(key, D, FF).astype(jnp.bfloat16)


def draw_down_codes(key, part):
    key = jax.random.fold_in(key, 13)
    return code_table(key, FF, D).astype(jnp.bfloat16)


def block_scale(own_key, dims, cuts, low, largest):
    factor_of = 1.0
    for dim, blocks in cuts:
        heights = jax.random.uniform(jax.random.fold_in(jax.random.fold_in(own_key, 6), dim), (blocks,), jnp.float32, low / len(cuts), largest / len(cuts))
        factor_of = factor_of * jnp.repeat(jnp.exp(heights), dims[dim] // blocks).reshape((-1,) + (1,) * (len(dims) - 1 - dim))
    return factor_of


def centred(rng, shape, deviation, reach, split=(), kind=jnp.bfloat16):
    values = deviation * jax.random.normal(rng, shape, jnp.float32)
    if split:
        values = values * block_scale(rng, shape, split, -0.22, 0.18)
    return jnp.clip(values, -reach, reach).astype(kind)


def setup_inputs(seed: int = 0) -> dict:
    seeds = jax.random.split(jax.random.key(seed), 14)
    return {
        "tokens": centred(seeds[0], (TOKENS, D), 1.0, 6.0, ((0, 16), (1, 8))),
        "gate_codes": draw_gate_codes(jax.random.fold_in(seeds[13], 71), 0),
        "up_codes": draw_up_codes(jax.random.fold_in(seeds[13], 71), 0),
        "gate_scale": jnp.clip(jnp.exp(math.log(0.003) - 1.2039728 * jax.random.uniform(seeds[3], (D // GROUP, FF), jnp.float32) ** block_scale(seeds[3], (D // GROUP, FF), ((0, 8), (1, 16)), -0.2, 0.2)), 0.0009, 0.003),
        "up_scale": jnp.clip(jnp.exp(math.log(0.003) - 1.2039728 * jax.random.uniform(seeds[4], (D // GROUP, FF), jnp.float32) ** block_scale(seeds[4], (D // GROUP, FF), ((0, 8), (1, 16)), -0.2, 0.2)), 0.0009, 0.003),
        "down_codes": draw_down_codes(jax.random.fold_in(seeds[13], 71), 0),
        "down_scale": jnp.clip(jnp.exp(math.log(0.0024) - 1.2321438 * jax.random.uniform(seeds[6], (FF // GROUP, D), jnp.float32) ** block_scale(seeds[6], (FF // GROUP, D), ((0, 16), (1, 8)), -0.2, 0.2)), 0.0007, 0.0024),
        "gate_left": centred(seeds[7], (D, RANK), D ** -0.5, 0.046875, ((0, 8),), jnp.float32),
        "gate_right": centred(seeds[8], (RANK, FF), RANK ** -0.5, 0.5, ((1, 16),), jnp.float32),
        "up_left": centred(seeds[9], (D, RANK), D ** -0.5, 0.046875, ((0, 8),), jnp.float32),
        "up_right": centred(seeds[10], (RANK, FF), RANK ** -0.5, 0.5, ((1, 16),), jnp.float32),
        "down_left": centred(seeds[11], (FF, RANK), FF ** -0.5, 0.0390625, ((0, 16),), jnp.float32),
        "down_right": centred(seeds[12], (RANK, D), RANK ** -0.5, 0.5, ((1, 8),), jnp.float32),
    }


def dequant(codes, scale):
    rows, cols = codes.shape
    groups = scale.shape[0]
    values = codes.astype(jnp.float32).reshape(groups, rows // groups, cols) * scale[:, None, :]
    return values.reshape(rows, cols).astype(jnp.bfloat16)


def reference(tokens, gate_codes, up_codes, gate_scale, up_scale, down_codes, down_scale, gate_left, gate_right, up_left, up_right, down_left, down_right):
    width = FF // N_WIDE
    highest = lax.Precision.HIGHEST
    tok_float = tokens.astype(jnp.float32)
    gate_low = jnp.dot(tok_float, gate_left, precision=highest)
    up_low = jnp.dot(tok_float, up_left, precision=highest)

    def step(carry, index):
        total, middle = carry
        first = (index * width).astype(jnp.int32)
        group_first = (index * (width // GROUP)).astype(jnp.int32)
        gate_w = dequant(lax.dynamic_slice_in_dim(gate_codes, first, width, 1), lax.dynamic_slice_in_dim(gate_scale, first, width, 1))
        up_w = dequant(lax.dynamic_slice_in_dim(up_codes, first, width, 1), lax.dynamic_slice_in_dim(up_scale, first, width, 1))
        gate = jnp.dot(tokens, gate_w, preferred_element_type=jnp.float32) + jnp.dot(gate_low, lax.dynamic_slice_in_dim(gate_right, first, width, 1), precision=highest)
        up = jnp.dot(tokens, up_w, preferred_element_type=jnp.float32) + jnp.dot(up_low, lax.dynamic_slice_in_dim(up_right, first, width, 1), precision=highest)
        hidden = (jax.nn.silu(gate) * up).astype(jnp.bfloat16)
        down_w = dequant(lax.dynamic_slice_in_dim(down_codes, first, width, 0), lax.dynamic_slice_in_dim(down_scale, group_first, width // GROUP, 0))
        total = total + jnp.dot(hidden, down_w, preferred_element_type=jnp.float32)
        middle = middle + jnp.dot(hidden.astype(jnp.float32), lax.dynamic_slice_in_dim(down_left, first, width, 0), precision=highest)
        return (total, middle), None

    start = (jnp.zeros((TOKENS, D), jnp.float32), jnp.zeros((TOKENS, RANK), jnp.float32))
    (total, middle), _ = lax.scan(step, start, jnp.arange(N_WIDE, dtype=jnp.int32))
    return total + jnp.dot(middle, down_right, precision=highest)
```

```python
import jax
import jax.numpy as jnp
from jax import lax
from jax.experimental import pallas as pl
from jax.experimental.pallas import tpu as pltpu
from jax.sharding import PartitionSpec as P

MESH = pl.DeviceIdType.MESH
F32 = jnp.float32
BF16 = jnp.bfloat16
LANE = 128
HALVES = 2
SKEW_SUM = 2
SKEW_DOWN = 5


def remote(src, dst, send_sem, recv_sem, device):
    return pltpu.make_async_remote_copy(
        src_ref=src,
        dst_ref=dst,
        send_sem=send_sem,
        recv_sem=recv_sem,
        device_id=device,
        device_id_type=MESH,
    )


def aligned(value, size):
    return pl.multiple_of(value, size)


def make_kernel(n_wide, n_narrow, depth, columns, tok_rows):
    blocks = columns // LANE
    units = HALVES * blocks
    chips = n_wide // 2
    part = tok_rows // HALVES
    core_rows = chips * part
    half_rows = 2 * core_rows
    own_rows = half_rows // n_narrow
    groups = depth // LANE
    wide_k = depth + 2 * LANE

    def kernel(
        tok, gate_codes, up_codes, gate_scale, up_scale, down_codes, down_scale,
        gate_left, gate_right, up_left, up_right, down_left, down_right,
        out,
        x_all, w_up, w_down, partial, landed, hidden, acc,
        core_send, core_land, out_send, out_land,
        scale_v, dscale_v, left_v, right_v, dleft_v, dright_v, left_b, dright_b,
        load_w, load_d, load_s,
        tok_send, tok_recv, pair_send, pair_recv,
        sum_send, sum_recv, hid_send, hid_recv,
        core_ss, core_rs, out_ss, out_rs,
    ):
        w = lax.axis_index("wide")
        n = lax.axis_index("narrow")
        chip, core = w // 2, lax.rem(w, 2)
        sibling = (chip * 2 + (1 - core), n)

        def wide_peer(d):
            return lax.rem(chip + d, chips)

        def narrow_peer(d):
            return lax.rem(n + d, n_narrow)

        small = [
            pltpu.make_async_copy(gate_left, left_v.at[0], load_s.at[0]),
            pltpu.make_async_copy(up_left, left_v.at[1], load_s.at[1]),
            pltpu.make_async_copy(gate_scale, scale_v.at[0], load_s.at[2]),
            pltpu.make_async_copy(up_scale, scale_v.at[1], load_s.at[3]),
            pltpu.make_async_copy(gate_right, right_v.at[0], load_s.at[4]),
            pltpu.make_async_copy(up_right, right_v.at[1], load_s.at[5]),
            pltpu.make_async_copy(down_scale, dscale_v, load_s.at[6]),
            pltpu.make_async_copy(down_left, dleft_v, load_s.at[7]),
            pltpu.make_async_copy(down_right, dright_v, load_s.at[8]),
        ]

        def cols_of(g):
            return pl.ds(aligned(g * LANE, LANE), LANE)

        def up_loads(g):
            return [
                pltpu.make_async_copy(
                    codes.at[:, cols_of(g)],
                    w_up.at[g, pl.ds(0, depth), pl.ds(i * LANE, LANE)],
                    load_w.at[i, g],
                )
                for i, codes in enumerate((gate_codes, up_codes))
            ]

        def down_load(g):
            return pltpu.make_async_copy(
                down_codes.at[cols_of(g), :],
                w_down.at[cols_of(g), pl.ds(0, depth)],
                load_d.at[g],
            )

        for copy in small[:6]:
            copy.start()

        @pl.loop(0, blocks)
        def _(g):
            for copy in up_loads(g):
                copy.start()

        for copy in small[6:]:
            copy.start()

        @pl.loop(0, blocks)
        def _(g):
            down_load(g).start()

        barrier = pltpu.get_barrier_semaphore()
        for d in range(1, n_narrow):
            pl.semaphore_signal(barrier, inc=1, device_id=(w, narrow_peer(d)), device_id_type=MESH)
        for d in range(1, chips):
            pl.semaphore_signal(
                barrier, inc=1, device_id=(wide_peer(d) * 2 + core, n), device_id_type=MESH
            )
        pl.semaphore_signal(barrier, inc=1, device_id=sibling, device_id_type=MESH)
        pl.semaphore_wait(barrier, n_narrow - 1 + chips - 1 + 1)

        base = core * core_rows
        feats = pl.ds(0, depth)
        place = pl.ds(aligned(base + chip * part, 16), part)
        for h in range(HALVES):
            for d in range(1, chips):
                remote(
                    tok.at[pl.ds(h * part, part), :],
                    x_all.at[h, place, feats],
                    tok_send.at[h],
                    tok_recv.at[h],
                    (wide_peer(d) * 2 + core, n),
                ).start()
        for h in range(HALVES):
            x_all[h, place, feats] = tok[pl.ds(h * part, part), :]
        acc[...] = jnp.zeros_like(acc)

        for copy in small[:6]:
            copy.wait()
        left_b[:, pl.ds(0, LANE)] = left_v[0].astype(BF16)
        left_b[:, pl.ds(LANE, LANE)] = left_v[1].astype(BF16)

        @pl.loop(0, blocks)
        def _(g):
            for copy in up_loads(g):
                copy.wait()
            for i in range(2):
                here = pl.ds(i * LANE, LANE)
                for k in range(groups):
                    rows = pl.ds(k * LANE, LANE)
                    scale = scale_v[i, pl.ds(k, 1), cols_of(g)]
                    w_up[g, rows, here] = (w_up[g, rows, here].astype(F32) * scale).astype(BF16)
                right = right_v[i, :, cols_of(g)].astype(BF16)
                w_up[g, pl.ds(depth + i * LANE, LANE), here] = right
                w_up[g, pl.ds(depth + (1 - i) * LANE, LANE), here] = jnp.zeros_like(right)

        for copy in small[6:]:
            copy.wait()
        dright_b[...] = dright_v[...].astype(BF16)

        @pl.loop(0, blocks)
        def _(g):
            down_load(g).wait()
            rows = cols_of(g)
            scale = dscale_v[pl.ds(g, 1), :]
            w_down[rows, feats] = (w_down[rows, feats].astype(F32) * scale).astype(BF16)
            w_down[rows, pl.ds(depth, LANE)] = dleft_v[rows, :].astype(BF16)

        def pair_copy(h):
            rows = x_all.at[h, pl.ds(aligned(base, core_rows), core_rows), feats]
            return remote(rows, rows, pair_send.at[h], pair_recv.at[h], sibling)

        def tokens_in(h):
            got = x_all.at[h, pl.ds(0, (chips - 1) * part), feats]
            remote(got, got, tok_send.at[h], tok_recv.at[h], sibling).wait_recv()
            pair_copy(h).start()

        def low_rank(h):
            pair_copy(h).wait_recv()
            x_all[h, :, pl.ds(depth, 2 * LANE)] = jnp.dot(
                x_all[h, :, feats], left_b[...], preferred_element_type=F32
            ).astype(BF16)

        def first(u):
            h, g = u // blocks, lax.rem(u, blocks)
            partial[u] = jnp.dot(x_all[h], w_up[g], preferred_element_type=F32).astype(BF16)
            for d in range(1, n_narrow):
                peer = narrow_peer(d)
                remote(
                    partial.at[u, pl.ds(aligned(peer * own_rows, own_rows), own_rows)],
                    landed.at[u, d - 1],
                    sum_send.at[u],
                    sum_recv.at[u],
                    (w, peer),
                ).start()

        mine = pl.ds(aligned(n * own_rows, own_rows), own_rows)

        def summed(u):
            remote(landed.at[u], landed.at[u], sum_send.at[u], sum_recv.at[u], sibling).wait()
            total = partial[u, mine, :].astype(F32)
            for d in range(n_narrow - 1):
                total = total + landed[u, d].astype(F32)
            gate, up = total[:, :LANE], total[:, LANE:]
            hidden[u, mine, :] = (gate / (1.0 + jnp.exp(-gate)) * up).astype(BF16)
            for d in range(1, n_narrow):
                remote(
                    hidden.at[u, mine],
                    hidden.at[u, mine],
                    hid_send.at[u],
                    hid_recv.at[u],
                    (w, narrow_peer(d)),
                ).start()

        def second(u):
            h, g = u // blocks, lax.rem(u, blocks)
            got = hidden.at[u, pl.ds(0, half_rows - own_rows)]
            remote(got, got, hid_send.at[u], hid_recv.at[u], sibling).wait()
            acc[h] += jnp.dot(hidden[u], w_down[cols_of(g), :], preferred_element_type=F32)

        ours = pl.ds(aligned(base, core_rows), core_rows)
        theirs = pl.ds(aligned((1 - core) * core_rows, core_rows), core_rows)

        def core_copy(h):
            return remote(core_send.at[h], core_land.at[h], core_ss.at[h], core_rs.at[h], sibling)

        def to_sibling(h):
            low = acc[h, :, pl.ds(depth, LANE)].astype(BF16)
            acc[h, :, feats] += jnp.dot(low, dright_b[...], preferred_element_type=F32)
            core_send[h] = acc[h, theirs, feats].astype(BF16)
            core_copy(h).start()

        def to_owners(h):
            core_copy(h).wait()
            both = acc[h, ours, feats] + core_land[h].astype(F32)
            acc[h, ours, feats] = both
            out_send[h] = both.astype(BF16)
            for d in range(1, chips):
                peer = wide_peer(d)
                remote(
                    out_send.at[h, pl.ds(aligned(peer * part, part), part)],
                    out_land.at[h, d - 1],
                    out_ss.at[h],
                    out_rs.at[h],
                    (peer * 2 + core, n),
                ).start()

        def finish(h):
            remote(out_land.at[h], out_land.at[h], out_ss.at[h], out_rs.at[h], sibling).wait()
            total = acc[h, place, feats]
            for d in range(chips - 1):
                total = total + out_land[h, d].astype(F32)
            out[pl.ds(h * part, part), :] = total

        for h in range(HALVES):
            tokens_in(h)
            if h == 0:
                low_rank(h)

        @pl.loop(0, units + SKEW_DOWN)
        def _(t):
            @pl.when(t == blocks - 1)
            def _():
                low_rank(1)

            @pl.when(t < units)
            def _():
                first(t)

            @pl.when((t >= SKEW_SUM) & (t < units + SKEW_SUM))
            def _():
                summed(t - SKEW_SUM)

            @pl.when(t >= SKEW_DOWN)
            def _():
                second(t - SKEW_DOWN)

            @pl.when(t == blocks - 1 + SKEW_DOWN)
            def _():
                to_sibling(0)

            @pl.when(t == blocks + 1 + SKEW_DOWN)
            def _():
                to_owners(0)

        to_sibling(1)
        finish(0)
        to_owners(1)
        finish(1)
        for h in range(HALVES):
            got = x_all.at[h, pl.ds(0, (chips - 1) * part), feats]
            remote(got, got, tok_send.at[h], tok_recv.at[h], sibling).wait_send()
            pair_copy(h).wait_send()

    vmem = pltpu.VMEM
    dma = pltpu.SemaphoreType.DMA
    scratch = [
        vmem((HALVES, half_rows, wide_k), BF16),
        vmem((blocks, wide_k, 2 * LANE), BF16),
        vmem((columns, depth + LANE), BF16),
        vmem((units, half_rows, 2 * LANE), BF16),
        vmem((units, n_narrow - 1, own_rows, 2 * LANE), BF16),
        vmem((units, half_rows, LANE), BF16),
        vmem((HALVES, half_rows, depth + LANE), F32),
        vmem((HALVES, core_rows, depth), BF16),
        vmem((HALVES, core_rows, depth), BF16),
        vmem((HALVES, core_rows, depth), BF16),
        vmem((HALVES, chips - 1, part, depth), BF16),
        vmem((2, groups, columns), F32),
        vmem((blocks, depth), F32),
        vmem((2, depth, LANE), F32),
        vmem((2, LANE, columns), F32),
        vmem((columns, LANE), F32),
        vmem((LANE, depth), F32),
        vmem((depth, 2 * LANE), BF16),
        vmem((LANE, depth), BF16),
        dma((2, blocks)),
        dma((blocks,)),
        dma((9,)),
        dma((HALVES,)), dma((HALVES,)), dma((HALVES,)), dma((HALVES,)),
        dma((units,)), dma((units,)), dma((units,)), dma((units,)),
        dma((HALVES,)), dma((HALVES,)), dma((HALVES,)), dma((HALVES,)),
    ]
    return kernel, scratch


def solution(mesh):
    n_wide, n_narrow = mesh.shape["wide"], mesh.shape["narrow"]

    def shards(tokens, gate_codes, up_codes, *rest):
        tok_rows = tokens.shape[0]
        depth, columns = gate_codes.shape
        kernel, scratch = make_kernel(n_wide, n_narrow, depth, columns, tok_rows)
        in_specs = [pl.BlockSpec(memory_space=pltpu.VMEM)] + [
            pl.BlockSpec(memory_space=pl.ANY)
        ] * 12
        return pl.pallas_call(
            kernel,
            out_shape=jax.ShapeDtypeStruct((tok_rows, depth), F32),
            in_specs=in_specs,
            out_specs=pl.BlockSpec(memory_space=pltpu.VMEM),
            scratch_shapes=scratch,
            compiler_params=pltpu.CompilerParams(
                collective_id=0, has_side_effects=True, vmem_limit_bytes=60 << 20
            ),
        )(tokens, gate_codes, up_codes, *rest)

    placed = (
        P("wide", "narrow"),
        P("narrow", "wide"),
        P("narrow", "wide"),
        P("narrow", "wide"),
        P("narrow", "wide"),
        P("wide", "narrow"),
        P("wide", "narrow"),
        P("narrow", None),
        P(None, "wide"),
        P("narrow", None),
        P(None, "wide"),
        P("wide", None),
        P(None, "narrow"),
    )
    return jax.shard_map(
        shards, mesh=mesh, in_specs=placed, out_specs=P("wide", "narrow"), check_vma=False
    )
```

```python
import jax
import jax.numpy as jnp
from jax import lax
from jax.experimental import pallas as pl
from jax.experimental.pallas import tpu as pltpu
from jax.sharding import PartitionSpec as P

MESH = pl.DeviceIdType.MESH
F32 = jnp.float32
BF16 = jnp.bfloat16
LANE = 128
HALVES = 2
CHUNKS = 4
UNITS = 7
X_FIRST = (1, 3, 5)
SKEW = (4, 8, 12, 16)


def remote(src, dst, send_sem, recv_sem, device):
    return pltpu.make_async_remote_copy(
        src_ref=src,
        dst_ref=dst,
        send_sem=send_sem,
        recv_sem=recv_sem,
        device_id=device,
        device_id_type=MESH,
    )


def aligned(value, size):
    return pl.multiple_of(value, size)


def make_kernel(n_wide, n_narrow, depth, columns, tok_rows):
    chips = n_wide // 2
    part = tok_rows // HALVES
    rows = chips * part
    ranks_x = n_narrow // 2
    own = rows // n_narrow
    groups = depth // LANE
    blocks = columns // LANE
    wide_k = depth + 2 * LANE
    block = 2 * LANE
    units = CHUNKS * UNITS
    last_block = (UNITS - 1) * block

    def kernel(
        tok, gate_codes, up_codes, gate_scale, up_scale, down_codes, down_scale,
        gate_left, gate_right, up_left, up_right, down_left, down_right,
        out,
        x_all, w_up, w_last, w_down, partial, land_1, land_2, half_sum, own_sum, hidden, acc,
        core_send, core_land, out_send, out_land,
        scale_v, dscale_v, left_v, right_v, dleft_v, dright_v, left_b, dright_b,
        load_w, load_d, load_s,
        tok_send, tok_recv, pair_send, pair_recv,
        ss_1, rs_1, ss_2, rs_2, hid_send, hid_recv_1, hid_recv_2,
        core_ss, core_rs, out_ss, out_rs,
    ):
        w = lax.axis_index("wide")
        n = lax.axis_index("narrow")
        chip, core = w // 2, lax.rem(w, 2)
        x, zh = n // 2, lax.rem(n, 2)
        sibling = (chip * 2 + (1 - core), n)
        z_peer = (w, x * 2 + (1 - zh))

        def wide_peer(d):
            return lax.rem(chip + d, chips)

        def x_peer(d):
            return lax.rem(x + d, ranks_x)

        small = [
            pltpu.make_async_copy(gate_left, left_v.at[0], load_s.at[0]),
            pltpu.make_async_copy(up_left, left_v.at[1], load_s.at[1]),
            pltpu.make_async_copy(gate_scale, scale_v.at[0], load_s.at[2]),
            pltpu.make_async_copy(up_scale, scale_v.at[1], load_s.at[3]),
            pltpu.make_async_copy(gate_right, right_v.at[0], load_s.at[4]),
            pltpu.make_async_copy(up_right, right_v.at[1], load_s.at[5]),
            pltpu.make_async_copy(down_scale, dscale_v, load_s.at[6]),
            pltpu.make_async_copy(down_left, dleft_v, load_s.at[7]),
            pltpu.make_async_copy(down_right, dright_v, load_s.at[8]),
        ]
        feats = pl.ds(0, depth)

        def cols_of(g, size=block):
            return pl.ds(aligned(g * block, size), size)

        def up_loads(g, target, size):
            return [
                pltpu.make_async_copy(
                    codes.at[:, cols_of(g, size)],
                    target.at[feats, pl.ds(i * size, size)],
                    load_w.at[i, g],
                )
                for i, codes in enumerate((gate_codes, up_codes))
            ]

        def down_load(g):
            here = pl.ds(aligned(g * LANE, LANE), LANE)
            return pltpu.make_async_copy(
                down_codes.at[here, :], w_down.at[here, feats], load_d.at[g]
            )

        with jax.named_scope("issue"):
            for copy in small[:6]:
                copy.start()

            @pl.loop(0, UNITS - 1)
            def _(g):
                for copy in up_loads(g, w_up.at[g], block):
                    copy.start()

            for copy in up_loads(UNITS - 1, w_last, LANE) + small[6:]:
                copy.start()

            @pl.loop(0, blocks)
            def _(g):
                down_load(g).start()

        with jax.named_scope("greet"):
            barrier = pltpu.get_barrier_semaphore()
            greet = [(wide_peer(d) * 2 + core, n) for d in range(1, chips)]
            greet += [(w, x_peer(d) * 2 + zh) for d in range(1, ranks_x)] + [z_peer, sibling]
            for device in greet:
                pl.semaphore_signal(barrier, inc=1, device_id=device, device_id_type=MESH)
            pl.semaphore_wait(barrier, len(greet))

        place = pl.ds(aligned(chip * part, part), part)

        def tokens_out(q):
            h, c = q // 2, q % 2

            @pl.when(core == c)
            def _():
                for d in range(1, chips):
                    remote(
                        tok.at[pl.ds(h * part, part), :],
                        x_all.at[q, place, feats],
                        tok_send.at[h],
                        tok_recv.at[h],
                        (wide_peer(d) * 2 + core, n),
                    ).start()
                x_all[q, place, feats] = tok[pl.ds(h * part, part), :]

        def pair_copy(q):
            both = x_all.at[q, :, feats]
            return remote(both, both, pair_send.at[q], pair_recv.at[q], sibling)

        def tokens_pair(q):
            h, c = q // 2, q % 2

            @pl.when(core == c)
            def _():
                got = x_all.at[q, pl.ds(0, (chips - 1) * part), feats]
                remote(got, got, tok_send.at[h], tok_recv.at[h], sibling).wait()
                pair_copy(q).start()

        def low_rank(q):
            @pl.when(core != q % 2)
            def _():
                pair_copy(q).wait_recv()

            x_all[q, :, pl.ds(depth, 2 * LANE)] = jnp.dot(
                x_all[q, :, feats], left_b[...], preferred_element_type=F32
            ).astype(BF16)

        def prepare():
            for copy in small[:6]:
                copy.wait()
            left_b[:, pl.ds(0, LANE)] = left_v[0].astype(BF16)
            left_b[:, pl.ds(LANE, LANE)] = left_v[1].astype(BF16)

            def widen(g, target, size):
                for copy in up_loads(g, target, size):
                    copy.wait()
                for i in range(2):
                    here = pl.ds(i * size, size)
                    for k in range(groups):
                        at = pl.ds(k * LANE, LANE)
                        scale = scale_v[i, pl.ds(k, 1), cols_of(g, size)]
                        target[at, here] = (target[at, here].astype(F32) * scale).astype(BF16)
                    right = right_v[i, :, cols_of(g, size)].astype(BF16)
                    target[pl.ds(depth + i * LANE, LANE), here] = right
                    target[pl.ds(depth + (1 - i) * LANE, LANE), here] = jnp.zeros_like(right)

            @pl.loop(0, UNITS - 1)
            def _(g):
                widen(g, w_up.at[g], block)

            widen(UNITS - 1, w_last, LANE)
            for copy in small[6:]:
                copy.wait()
            dright_b[...] = dright_v[...].astype(BF16)

            @pl.loop(0, blocks)
            def _(g):
                down_load(g).wait()
                here = pl.ds(aligned(g * LANE, LANE), LANE)
                scale = dscale_v[pl.ds(g, 1), :]
                w_down[here, feats] = (w_down[here, feats].astype(F32) * scale).astype(BF16)
                w_down[here, pl.ds(depth, LANE)] = dleft_v[here, :].astype(BF16)

        def variants(stage):
            def run(u):
                q, g = u // UNITS, lax.rem(u, UNITS)
                along_x = g == X_FIRST[0]
                for other in X_FIRST[1:]:
                    along_x = along_x | (g == other)
                narrow_block = g == UNITS - 1

                @pl.when(along_x)
                def _():
                    stage(u, q, g, True, block)

                @pl.when(jnp.logical_not(along_x | narrow_block))
                def _():
                    stage(u, q, g, False, block)

                @pl.when(narrow_block)
                def _():
                    stage(u, q, g, False, LANE)

            return run

        def start_of(x_first, xi, zi):
            return aligned(xi * 2 * own + zi * own if x_first else zi * ranks_x * own + xi * own, own)

        def bytes_of(buffer, u, count, size, send, recv):
            at = buffer.at[u, pl.ds(0, count), pl.ds(0, size)]
            return remote(at, at, send.at[u], recv.at[u], sibling)

        def wait_1(u, x_first, size):
            count = (ranks_x - 1) * 2 * own if x_first else ranks_x * own
            return bytes_of(land_1, u, count, size, ss_1, rs_1)

        def wait_2(u, x_first, size):
            count = own if x_first else (ranks_x - 1) * own
            return bytes_of(land_2, u, count, size, ss_2, rs_2)

        def first(u, q, g, x_first, size):
            cols = pl.ds(0, 2 * size)
            weights = w_up[g] if size == block else w_last[...]
            partial[u, :, cols] = jnp.dot(
                x_all[q], weights, preferred_element_type=F32
            ).astype(BF16)
            if x_first:
                for d in range(1, ranks_x):
                    xi = x_peer(d)
                    remote(
                        partial.at[u, pl.ds(start_of(True, xi, 0), 2 * own), cols],
                        land_1.at[u, pl.ds((d - 1) * 2 * own, 2 * own), cols],
                        ss_1.at[u],
                        rs_1.at[u],
                        (w, xi * 2 + zh),
                    ).start()
            else:
                remote(
                    partial.at[u, pl.ds(start_of(False, 0, 1 - zh), ranks_x * own), cols],
                    land_1.at[u, pl.ds(0, ranks_x * own), cols],
                    ss_1.at[u],
                    rs_1.at[u],
                    z_peer,
                ).start()

        def sum_1(u, q, g, x_first, size):
            cols = pl.ds(0, 2 * size)
            wait_1(u, x_first, 2 * size).wait_recv()
            if x_first:

                def total(zi):
                    value = partial[u, pl.ds(start_of(True, x, zi), own), cols].astype(F32)
                    for d in range(ranks_x - 1):
                        at = pl.ds(aligned(d * 2 * own + zi * own, own), own)
                        value = value + land_1[u, at, cols].astype(F32)
                    return value

                half_sum[u, pl.ds(0, own), cols] = total(1 - zh).astype(BF16)
                remote(
                    half_sum.at[u, pl.ds(0, own), cols],
                    land_2.at[u, pl.ds(0, own), cols],
                    ss_2.at[u],
                    rs_2.at[u],
                    z_peer,
                ).start()
                own_sum[u, :, cols] = total(zh)
            else:
                group = pl.ds(start_of(False, 0, zh), ranks_x * own)
                got = pl.ds(0, ranks_x * own)
                half_sum[u, got, cols] = (
                    partial[u, group, cols].astype(F32) + land_1[u, got, cols].astype(F32)
                ).astype(BF16)
                for d in range(1, ranks_x):
                    xi = x_peer(d)
                    remote(
                        half_sum.at[u, pl.ds(aligned(xi * own, own), own), cols],
                        land_2.at[u, pl.ds((d - 1) * own, own), cols],
                        ss_2.at[u],
                        rs_2.at[u],
                        (w, xi * 2 + zh),
                    ).start()
                mine = pl.ds(aligned(x * own, own), own)
                own_sum[u, :, cols] = (
                    partial[u, pl.ds(start_of(False, x, zh), own), cols].astype(F32)
                    + land_1[u, mine, cols].astype(F32)
                )

        def hidden_copy(u, at, size, recv, device):
            here = hidden.at[u, at, pl.ds(0, size)]
            return remote(here, here, hid_send.at[u], recv.at[u], device)

        def sum_2(u, q, g, x_first, size):
            wait_2(u, x_first, 2 * size).wait_recv()
            total = own_sum[u, :, pl.ds(0, 2 * size)]
            for d in range(1 if x_first else ranks_x - 1):
                total = total + land_2[u, pl.ds(d * own, own), pl.ds(0, 2 * size)].astype(F32)
            gate, up = total[:, :size], total[:, size:]
            mine = pl.ds(start_of(x_first, x, zh), own)
            hidden[u, mine, pl.ds(0, size)] = (gate / (1.0 + jnp.exp(-gate)) * up).astype(BF16)
            along_z = hid_recv_1 if x_first else hid_recv_2
            along_x = hid_recv_2 if x_first else hid_recv_1
            hidden_copy(u, mine, size, along_z, z_peer).start()
            for d in range(1, ranks_x):
                hidden_copy(u, mine, size, along_x, (w, x_peer(d) * 2 + zh)).start()

        def wait_early(u, x_first, size):
            count = own if x_first else (ranks_x - 1) * own
            return bytes_of(hidden, u, count, size, hid_send, hid_recv_1)

        def wait_late(u, x_first, size):
            count = (ranks_x - 1) * 2 * own if x_first else ranks_x * own
            return bytes_of(hidden, u, count, size, hid_send, hid_recv_2)

        def relay(u, q, g, x_first, size):
            wait_early(u, x_first, size).wait_recv()
            for d in range(1, ranks_x):
                xi = x_peer(d)
                if x_first:
                    at = pl.ds(start_of(True, x, 1 - zh), own)
                    device = (w, xi * 2 + zh)
                else:
                    at = pl.ds(start_of(False, xi, zh), own)
                    device = z_peer
                hidden_copy(u, at, size, hid_recv_2, device).start()

        def second(u, q, g, x_first, size):
            wait_late(u, x_first, size).wait_recv()
            acc[q] += jnp.dot(
                hidden[u, :, pl.ds(0, size)],
                w_down[cols_of(g, size), :],
                preferred_element_type=F32,
            )
            wait_1(u, x_first, 2 * size).wait_send()
            wait_2(u, x_first, 2 * size).wait_send()
            bytes_of(hidden, u, (n_narrow - 1) * own, size, hid_send, hid_recv_2).wait_send()

        def core_copy(h):
            return remote(core_send.at[h], core_land.at[h], core_ss.at[h], core_rs.at[h], sibling)

        def to_owning_core(q):
            low = acc[q, :, pl.ds(depth, LANE)].astype(BF16)
            acc[q, :, feats] += jnp.dot(low, dright_b[...], preferred_element_type=F32)

            @pl.when(core != q % 2)
            def _():
                core_send[q // 2] = acc[q, :, feats].astype(BF16)
                core_copy(q // 2).start()

        def to_owners(q):
            h = q // 2

            @pl.when(core == q % 2)
            def _():
                core_copy(h).wait_recv()
                both = acc[q, :, feats] + core_land[h].astype(F32)
                acc[q, :, feats] = both
                out_send[h] = both.astype(BF16)
                for d in range(1, chips):
                    peer = wide_peer(d)
                    remote(
                        out_send.at[h, pl.ds(aligned(peer * part, part), part)],
                        out_land.at[h, d - 1],
                        out_ss.at[h],
                        out_rs.at[h],
                        (peer * 2 + core, n),
                    ).start()

        def finish(q):
            h = q // 2

            @pl.when(core == q % 2)
            def _():
                remote(out_land.at[h], out_land.at[h], out_ss.at[h], out_rs.at[h], sibling).wait()
                total = acc[q, place, feats]
                for d in range(chips - 1):
                    total = total + out_land[h, d].astype(F32)
                out[pl.ds(h * part, part), :] = total
                pair_copy(q).wait_send()

            @pl.when(core != q % 2)
            def _():
                core_copy(h).wait_send()

        def scope(name, function, *given):
            with jax.named_scope(name):
                function(*given)

        scope("tokens_out", tokens_out, 0)
        acc[...] = jnp.zeros_like(acc)
        scope("prepare", prepare)
        scope("tokens_out", tokens_out, 1)
        scope("tokens_pair", tokens_pair, 0)
        scope("low_rank", low_rank, 0)

        events = {}
        for q in range(1, CHUNKS):
            if q > 1:
                events.setdefault(UNITS * (q - 2) + 1, []).append(("tokens_out", tokens_out, q))
            events.setdefault(UNITS * q - 4, []).append(("tokens_pair", tokens_pair, q))
            events.setdefault(UNITS * q - 1, []).append(("low_rank", low_rank, q))
        for q in range(CHUNKS - 1):
            done = UNITS * (q + 1) - 1 + SKEW[3]
            events.setdefault(done, []).append(("to_owning_core", to_owning_core, q))
            events.setdefault(done + 2, []).append(("to_owners", to_owners, q))
        stages = [("first", 0, variants(first))]
        for name, skew, stage in zip(
            ("sum_1", "sum_2", "relay", "second"), SKEW, (sum_1, sum_2, relay, second)
        ):
            stages.append((name, skew, variants(stage)))

        @pl.loop(0, units + SKEW[3])
        def _(t):
            for name, skew, stage in stages:

                @pl.when((t >= skew) & (t < units + skew))
                def _():
                    scope(name, stage, t - skew)

            for at, todo in events.items():

                @pl.when(t == at)
                def _():
                    for name, function, q in todo:
                        scope(name, function, q)

        scope("to_owning_core", to_owning_core, CHUNKS - 1)
        for q in range(CHUNKS - 2):
            scope("finish", finish, q)
        scope("to_owners", to_owners, CHUNKS - 1)
        for q in range(CHUNKS - 2, CHUNKS):
            scope("finish", finish, q)

    vmem = pltpu.VMEM
    dma = pltpu.SemaphoreType.DMA
    scratch = [
        vmem((CHUNKS, rows, wide_k), BF16),
        vmem((UNITS - 1, wide_k, 2 * block), BF16),
        vmem((wide_k, block), BF16),
        vmem((columns, depth + LANE), BF16),
        vmem((units, rows, 2 * block), BF16),
        vmem((units, (ranks_x - 1) * 2 * own, 2 * block), BF16),
        vmem((units, (ranks_x - 1) * own, 2 * block), BF16),
        vmem((units, ranks_x * own, 2 * block), BF16),
        vmem((units, own, 2 * block), F32),
        vmem((units, rows, block), BF16),
        vmem((CHUNKS, rows, depth + LANE), F32),
        vmem((HALVES, rows, depth), BF16),
        vmem((HALVES, rows, depth), BF16),
        vmem((HALVES, rows, depth), BF16),
        vmem((HALVES, chips - 1, part, depth), BF16),
        vmem((2, groups, columns), F32),
        vmem((blocks, depth), F32),
        vmem((2, depth, LANE), F32),
        vmem((2, LANE, columns), F32),
        vmem((columns, LANE), F32),
        vmem((LANE, depth), F32),
        vmem((depth, 2 * LANE), BF16),
        vmem((LANE, depth), BF16),
        dma((2, UNITS)),
        dma((blocks,)),
        dma((9,)),
        dma((HALVES,)), dma((HALVES,)), dma((CHUNKS,)), dma((CHUNKS,)),
        dma((units,)), dma((units,)), dma((units,)), dma((units,)),
        dma((units,)), dma((units,)), dma((units,)),
        dma((HALVES,)), dma((HALVES,)), dma((HALVES,)), dma((HALVES,)),
    ]
    return kernel, scratch


def solution(mesh):
    n_wide, n_narrow = mesh.shape["wide"], mesh.shape["narrow"]

    def shards(tokens, gate_codes, up_codes, *rest):
        tok_rows = tokens.shape[0]
        depth, columns = gate_codes.shape
        kernel, scratch = make_kernel(n_wide, n_narrow, depth, columns, tok_rows)
        in_specs = [pl.BlockSpec(memory_space=pltpu.VMEM)] + [
            pl.BlockSpec(memory_space=pl.ANY)
        ] * 12
        return pl.pallas_call(
            kernel,
            out_shape=jax.ShapeDtypeStruct((tok_rows, depth), F32),
            in_specs=in_specs,
            out_specs=pl.BlockSpec(memory_space=pltpu.VMEM),
            scratch_shapes=scratch,
            compiler_params=pltpu.CompilerParams(
                collective_id=0, has_side_effects=True, vmem_limit_bytes=60 << 20
            ),
        )(tokens, gate_codes, up_codes, *rest)

    placed = (
        P("wide", "narrow"),
        P("narrow", "wide"),
        P("narrow", "wide"),
        P("narrow", "wide"),
        P("narrow", "wide"),
        P("wide", "narrow"),
        P("wide", "narrow"),
        P("narrow", None),
        P(None, "wide"),
        P("narrow", None),
        P(None, "wide"),
        P("wide", None),
        P(None, "narrow"),
    )
    return jax.shard_map(
        shards, mesh=mesh, in_specs=placed, out_specs=P("wide", "narrow"), check_vma=False
    )
```

```python
import jax
import jax.numpy as jnp
from jax import lax
from jax.experimental import pallas as pl
from jax.experimental.pallas import tpu as pltpu
from jax.sharding import PartitionSpec as P

MESH = pl.DeviceIdType.MESH
F32 = jnp.float32
BF16 = jnp.bfloat16
LANE = 128
HALVES = 2
CHUNKS = 4
UNITS = 7
X_FIRST = (1, 3, 5)
SKEW = (4, 8, 12, 16)
AFTER = (3, 9)
OUT_AT = (-1, 0, 3)
RELAY_AT = (-1, 4, 10)
PAIR_AT = (1, 9, 16)
SPREAD = 3


def remote(src, dst, send_sem, recv_sem, device):
    return pltpu.make_async_remote_copy(
        src_ref=src,
        dst_ref=dst,
        send_sem=send_sem,
        recv_sem=recv_sem,
        device_id=device,
        device_id_type=MESH,
    )


def aligned(value, size):
    return pl.multiple_of(value, size)


def make_kernel(n_wide, n_narrow, depth, columns, tok_rows):
    chips = n_wide // 2
    ranks_y = chips // 2
    part = tok_rows // HALVES
    rows = chips * part
    ranks_x = n_narrow // 2
    own = rows // n_narrow
    groups = depth // LANE
    blocks = columns // LANE
    wide_k = depth + 2 * LANE
    block = 2 * LANE
    units = CHUNKS * UNITS
    last_block = (UNITS - 1) * block

    def kernel(
        tok, gate_codes, up_codes, gate_scale, up_scale, down_codes, down_scale,
        gate_left, gate_right, up_left, up_right, down_left, down_right,
        out,
        x_all, w_up, w_last, w_down, partial, land_1, land_2, half_sum, own_sum, hidden, acc,
        core_send, core_land, out_send, out_land, z_send, z_land,
        scale_v, dscale_v, left_v, right_v, dleft_v, dright_v, left_b, dright_b,
        load_w, load_d, load_s,
        tok_send, tok_first, tok_recv, tok_recv_z, pair_send, pair_recv,
        ss_1, rs_1, ss_2, rs_2, hid_send, hid_recv_1, hid_recv_2,
        core_ss, core_rs, out_ss, out_rs, z_ss, z_rs,
    ):
        w = lax.axis_index("wide")
        n = lax.axis_index("narrow")
        core, y, zl = lax.rem(w, 2), lax.rem(w // 2, ranks_y), w // chips
        x, zh = n // 2, lax.rem(n, 2)
        sibling = (w + 1 - 2 * core, n)
        z_peer = (w, x * 2 + (1 - zh))

        def y_peer(d):
            return lax.rem(y + d, ranks_y)

        def chip_at(yi, zi):
            return (zi * chips + yi * 2 + core, n)

        def tok_place(yi, zi, count=1):
            return pl.ds(aligned((yi * 2 + zi) * part, part), count * part)

        def x_peer(d):
            return lax.rem(x + d, ranks_x)

        small = [
            pltpu.make_async_copy(gate_left, left_v.at[0], load_s.at[0]),
            pltpu.make_async_copy(up_left, left_v.at[1], load_s.at[1]),
            pltpu.make_async_copy(gate_scale, scale_v.at[0], load_s.at[2]),
            pltpu.make_async_copy(up_scale, scale_v.at[1], load_s.at[3]),
            pltpu.make_async_copy(gate_right, right_v.at[0], load_s.at[4]),
            pltpu.make_async_copy(up_right, right_v.at[1], load_s.at[5]),
            pltpu.make_async_copy(down_scale, dscale_v, load_s.at[6]),
            pltpu.make_async_copy(down_left, dleft_v, load_s.at[7]),
            pltpu.make_async_copy(down_right, dright_v, load_s.at[8]),
        ]
        feats = pl.ds(0, depth)

        def cols_of(g, size=block):
            return pl.ds(aligned(g * block, size), size)

        def up_loads(g, target, size):
            return [
                pltpu.make_async_copy(
                    codes.at[:, cols_of(g, size)],
                    target.at[feats, pl.ds(i * size, size)],
                    load_w.at[i, g],
                )
                for i, codes in enumerate((gate_codes, up_codes))
            ]

        def down_load(g):
            here = pl.ds(aligned(g * LANE, LANE), LANE)
            return pltpu.make_async_copy(
                down_codes.at[here, :], w_down.at[here, feats], load_d.at[g]
            )

        with jax.named_scope("issue"):
            for copy in small[:6]:
                copy.start()

            @pl.loop(0, UNITS - 1)
            def _(g):
                for copy in up_loads(g, w_up.at[g], block):
                    copy.start()

            for copy in up_loads(UNITS - 1, w_last, LANE) + small[6:]:
                copy.start()

            @pl.loop(0, blocks)
            def _(g):
                down_load(g).start()

        with jax.named_scope("greet"):
            barrier = pltpu.get_barrier_semaphore()
            greet = [chip_at(y_peer(d), zi) for d in range(1, ranks_y) for zi in range(2)]
            greet += [chip_at(y, 1 - zl)]
            greet += [(w, x_peer(d) * 2 + zi) for d in range(1, ranks_x) for zi in range(2)]
            greet += [z_peer, sibling]
            for device in greet:
                pl.semaphore_signal(barrier, inc=1, device_id=device, device_id_type=MESH)
            pl.semaphore_wait(barrier, len(greet))

        place = tok_place(y, zl)

        def tokens_out(q):
            h, c = q // 2, q % 2

            @pl.when(core == c)
            def _():
                def send(recv, device):
                    remote(
                        tok.at[pl.ds(h * part, part), :],
                        x_all.at[q, place, feats],
                        tok_send.at[h],
                        recv,
                        device,
                    ).start()

                send(tok_first.at[0] if q == 0 else tok_recv_z.at[h], chip_at(y, 1 - zl))
                for d in range(1, ranks_y):
                    send(tok_first.at[d] if q == 0 else tok_recv.at[h], chip_at(y_peer(d), zl))
                    if q == 0:
                        send(tok_first.at[ranks_y - 1 + d], chip_at(y_peer(d), 1 - zl))
                x_all[q, place, feats] = tok[pl.ds(h * part, part), :]

        def tokens_got(q, count, recv):
            got = x_all.at[q, pl.ds(0, count * part), feats]
            return remote(got, got, tok_send.at[q // 2], recv.at[q // 2], sibling)

        def tokens_relay(q):
            @pl.when(core == q % 2)
            def _():
                tokens_got(q, 1, tok_recv_z).wait_recv()
                here = x_all.at[q, tok_place(y, 1 - zl), feats]
                for d in range(1, ranks_y):
                    remote(
                        here, here, tok_send.at[q // 2], tok_recv.at[q // 2], chip_at(y_peer(d), zl)
                    ).start()

        def pair_copy(q):
            both = x_all.at[q, :, feats]
            return remote(both, both, pair_send.at[q], pair_recv.at[q], sibling)

        def pass_on(at):
            here = x_all.at[0, at, feats]
            remote(here, here, pair_send.at[0], pair_recv.at[0], sibling).start()

        def tokens_pair(q):
            @pl.when(core == q % 2)
            def _():
                if q > 0:
                    tokens_got(q, chips - 2, tok_recv).wait_recv()
                    pair_copy(q).start()
                else:
                    pass_on(place)
                    for d in (0, 1, 3, 4, 6, 2, 5):
                        side = 0 if d == 0 else (d - 1) % (ranks_y - 1) + 1
                        yi = lax.rem(y + ranks_y - side, ranks_y)
                        here = tok_place(yi, zl if 0 < d < ranks_y else 1 - zl)
                        got = x_all.at[q, here, feats]
                        remote(got, got, tok_send.at[0], tok_first.at[d], sibling).wait_recv()
                        pass_on(here)
                tokens_got(q, chips - 1, tok_recv).wait_send()

        def low_rank(q):
            @pl.when(core != q % 2)
            def _():
                pair_copy(q).wait_recv()

            x_all[q, :, pl.ds(depth, 2 * LANE)] = jnp.dot(
                x_all[q, :, feats], left_b[...], preferred_element_type=F32
            ).astype(BF16)

        def prepare():
            for copy in small[:6]:
                copy.wait()
            left_b[:, pl.ds(0, LANE)] = left_v[0].astype(BF16)
            left_b[:, pl.ds(LANE, LANE)] = left_v[1].astype(BF16)

            def widen(g, target, size):
                for copy in up_loads(g, target, size):
                    copy.wait()
                for i in range(2):
                    here = pl.ds(i * size, size)
                    for k in range(groups):
                        at = pl.ds(k * LANE, LANE)
                        scale = scale_v[i, pl.ds(k, 1), cols_of(g, size)]
                        target[at, here] = (target[at, here].astype(F32) * scale).astype(BF16)
                    right = right_v[i, :, cols_of(g, size)].astype(BF16)
                    target[pl.ds(depth + i * LANE, LANE), here] = right
                    target[pl.ds(depth + (1 - i) * LANE, LANE), here] = jnp.zeros_like(right)

            @pl.loop(0, UNITS - 1)
            def _(g):
                widen(g, w_up.at[g], block)

            widen(UNITS - 1, w_last, LANE)
            for copy in small[6:]:
                copy.wait()
            dright_b[...] = dright_v[...].astype(BF16)

            @pl.loop(0, blocks)
            def _(g):
                down_load(g).wait()
                here = pl.ds(aligned(g * LANE, LANE), LANE)
                scale = dscale_v[pl.ds(g, 1), :]
                w_down[here, feats] = (w_down[here, feats].astype(F32) * scale).astype(BF16)
                w_down[here, pl.ds(depth, LANE)] = dleft_v[here, :].astype(BF16)

        def run(stage, q, g):
            stage(q * UNITS + g, q, g, g in X_FIRST, LANE if g == UNITS - 1 else block)

        def start_of(x_first, xi, zi):
            return aligned(xi * 2 * own + zi * own if x_first else zi * ranks_x * own + xi * own, own)

        def bytes_of(buffer, u, count, size, send, recv):
            at = buffer.at[u, pl.ds(0, count), pl.ds(0, size)]
            return remote(at, at, send.at[u], recv.at[u], sibling)

        def wait_1(u, x_first, size):
            count = (ranks_x - 1) * 2 * own if x_first else ranks_x * own
            return bytes_of(land_1, u, count, size, ss_1, rs_1)

        def wait_2(u, x_first, size):
            count = own if x_first else (ranks_x - 1) * own
            return bytes_of(land_2, u, count, size, ss_2, rs_2)

        def first(u, q, g, x_first, size):
            cols = pl.ds(0, 2 * size)
            weights = w_up[g] if size == block else w_last[...]
            partial[u, :, cols] = jnp.dot(
                x_all[q], weights, preferred_element_type=F32
            ).astype(BF16)
            if x_first:
                for d in range(1, ranks_x):
                    xi = x_peer(d)
                    remote(
                        partial.at[u, pl.ds(start_of(True, xi, 0), 2 * own), cols],
                        land_1.at[u, pl.ds((d - 1) * 2 * own, 2 * own), cols],
                        ss_1.at[u],
                        rs_1.at[u],
                        (w, xi * 2 + zh),
                    ).start()
            else:
                remote(
                    partial.at[u, pl.ds(start_of(False, 0, 1 - zh), ranks_x * own), cols],
                    land_1.at[u, pl.ds(0, ranks_x * own), cols],
                    ss_1.at[u],
                    rs_1.at[u],
                    z_peer,
                ).start()

        def hidden_copy(u, at, size, recv, device):
            here = hidden.at[u, at, pl.ds(0, size)]
            return remote(here, here, hid_send.at[u], recv.at[u], device)

        def activate(u, q, total, x_first, size):
            gate, up = total[:, :size], total[:, size:]
            mine = pl.ds(start_of(x_first, x, zh), own)
            hidden[u, mine, pl.ds(0, size)] = (gate / (1.0 + jnp.exp(-gate)) * up).astype(BF16)
            along_z = hid_recv_1 if x_first else hid_recv_2
            along_x = hid_recv_2 if x_first else hid_recv_1
            hidden_copy(u, mine, size, along_z, z_peer).start()
            for d in range(1, ranks_x):
                xi = x_peer(d) * 2
                hidden_copy(u, mine, size, along_x, (w, xi + zh)).start()

            @pl.when(q >= SPREAD)
            def _():
                for d in range(1, ranks_x):
                    device = (w, x_peer(d) * 2 + 1 - zh)
                    hidden_copy(u, mine, size, hid_recv_2, device).start()

        def sum_1(u, q, g, x_first, size):
            cols = pl.ds(0, 2 * size)
            wait_1(u, x_first, 2 * size).wait_recv()
            if x_first:

                def total(zi):
                    value = partial[u, pl.ds(start_of(True, x, zi), own), cols].astype(F32)
                    for d in range(ranks_x - 1):
                        at = pl.ds(aligned(d * 2 * own + zi * own, own), own)
                        value = value + land_1[u, at, cols].astype(F32)
                    return value

                half_sum[u, pl.ds(0, own), cols] = total(1 - zh).astype(BF16)
                remote(
                    half_sum.at[u, pl.ds(0, own), cols],
                    land_2.at[u, pl.ds(0, own), cols],
                    ss_2.at[u],
                    rs_2.at[u],
                    z_peer,
                ).start()
                own_sum[u, :, cols] = total(zh)
            else:
                group = pl.ds(start_of(False, 0, zh), ranks_x * own)
                got = pl.ds(0, ranks_x * own)
                half_sum[u, got, cols] = (
                    partial[u, group, cols].astype(F32) + land_1[u, got, cols].astype(F32)
                ).astype(BF16)
                for d in range(1, ranks_x):
                    xi = x_peer(d)
                    remote(
                        half_sum.at[u, pl.ds(aligned(xi * own, own), own), cols],
                        land_2.at[u, pl.ds((d - 1) * own, own), cols],
                        ss_2.at[u],
                        rs_2.at[u],
                        (w, xi * 2 + zh),
                    ).start()
                mine = pl.ds(aligned(x * own, own), own)
                own_sum[u, :, cols] = (
                    partial[u, pl.ds(start_of(False, x, zh), own), cols].astype(F32)
                    + land_1[u, mine, cols].astype(F32)
                )

        def sum_2(u, q, g, x_first, size):
            wait_2(u, x_first, 2 * size).wait_recv()
            total = own_sum[u, :, pl.ds(0, 2 * size)]
            for d in range(1 if x_first else ranks_x - 1):
                total = total + land_2[u, pl.ds(d * own, own), pl.ds(0, 2 * size)].astype(F32)
            activate(u, q, total, x_first, size)

        def wait_early(u, x_first, size):
            count = own if x_first else (ranks_x - 1) * own
            return bytes_of(hidden, u, count, size, hid_send, hid_recv_1)

        def wait_late(u, x_first, size):
            count = (ranks_x - 1) * 2 * own if x_first else ranks_x * own
            return bytes_of(hidden, u, count, size, hid_send, hid_recv_2)

        def relay(u, q, g, x_first, size):
            wait_early(u, x_first, size).wait_recv()

            @pl.when(q < SPREAD)
            def _():
                for d in range(1, ranks_x):
                    xi = x_peer(d)
                    if x_first:
                        at = pl.ds(start_of(True, x, 1 - zh), own)
                        device = (w, xi * 2 + zh)
                    else:
                        at = pl.ds(start_of(False, xi, zh), own)
                        device = z_peer
                    hidden_copy(u, at, size, hid_recv_2, device).start()

        def second(u, q, g, x_first, size):
            wait_late(u, x_first, size).wait_recv()
            acc[q] += jnp.dot(
                hidden[u, :, pl.ds(0, size)],
                w_down[cols_of(g, size), :],
                preferred_element_type=F32,
            )
            wait_1(u, x_first, 2 * size).wait_send()
            wait_2(u, x_first, 2 * size).wait_send()
            bytes_of(hidden, u, (n_narrow - 1) * own, size, hid_send, hid_recv_2).wait_send()

        def core_copy(h):
            return remote(core_send.at[h], core_land.at[h], core_ss.at[h], core_rs.at[h], sibling)

        def to_owning_core(q):
            low = acc[q, :, pl.ds(depth, LANE)].astype(BF16)
            acc[q, :, feats] += jnp.dot(low, dright_b[...], preferred_element_type=F32)

            @pl.when(core != q % 2)
            def _():
                core_send[q // 2] = acc[q, :, feats].astype(BF16)
                core_copy(q // 2).start()

        def out_copy(h, src, dst, send, recv, device):
            return remote(src, dst, send.at[h], recv.at[h], device)

        def to_owners(q):
            h = q // 2

            @pl.when(core == q % 2)
            def _():
                core_copy(h).wait_recv()
                both = acc[q, :, feats] + core_land[h].astype(F32)
                acc[q, :, feats] = both
                out_send[h] = both.astype(BF16)
                for d in range(1, ranks_y):
                    yi = y_peer(d)
                    if q < CHUNKS - 1:
                        at = pl.ds((d - 1) * 2 * part, 2 * part)
                        remote(
                            out_send.at[h, tok_place(yi, 0, 2)],
                            out_land.at[h, at],
                            out_ss.at[h],
                            out_rs.at[h],
                            chip_at(yi, zl),
                        ).start()
                        continue
                    for zi in range(2):
                        at = pl.ds(aligned(((d - 1) * 2 + zl) * part, part), part)
                        remote(
                            out_send.at[h, tok_place(yi, zi)],
                            out_land.at[h, at],
                            out_ss.at[h],
                            out_rs.at[h],
                            chip_at(yi, zi),
                        ).start()
                if q == CHUNKS - 1:
                    remote(
                        out_send.at[h, tok_place(y, 1 - zl)],
                        z_land.at[h],
                        z_ss.at[h],
                        z_rs.at[h],
                        chip_at(y, 1 - zl),
                    ).start()

        def out_wait(h):
            got = out_land.at[h]
            return remote(got, got, out_ss.at[h], out_rs.at[h], sibling)

        def z_copy(h):
            return remote(z_send.at[h], z_land.at[h], z_ss.at[h], z_rs.at[h], chip_at(y, 1 - zl))

        def to_z(q):
            h = q // 2

            @pl.when(core == q % 2)
            def _():
                out_wait(h).wait()

                def total(zi):
                    value = acc[q, tok_place(y, zi), feats]
                    for d in range(ranks_y - 1):
                        at = pl.ds(aligned((d * 2 + zi) * part, part), part)
                        value = value + out_land[h, at].astype(F32)
                    return value

                z_send[h] = total(1 - zl).astype(BF16)
                z_copy(h).start()
                acc[q, place, feats] = total(zl)

        def finish(q):
            h = q // 2

            @pl.when(core == q % 2)
            def _():
                total = acc[q, place, feats]
                if q == CHUNKS - 1:
                    out_wait(h).wait()
                    for d in range((ranks_y - 1) * 2):
                        total = total + out_land[h, pl.ds(d * part, part)].astype(F32)
                z_copy(h).wait()
                out[pl.ds(h * part, part), :] = total + z_land[h].astype(F32)
                pair_copy(q).wait_send()

            @pl.when(core != q % 2)
            def _():
                core_copy(h).wait_send()

        def scope(name, function, *given):
            with jax.named_scope(name):
                function(*given)

        scope("tokens_out", tokens_out, 0)
        acc[...] = jnp.zeros_like(acc)
        scope("prepare", prepare)
        if OUT_AT[0] < 0:
            scope("tokens_out", tokens_out, 1)
        scope("tokens_pair", tokens_pair, 0)
        if RELAY_AT[0] < 0:
            scope("tokens_relay", tokens_relay, 1)
        scope("low_rank", low_rank, 0)

        events = {}
        for q in range(1, CHUNKS):
            if OUT_AT[q - 1] >= 0:
                events.setdefault(OUT_AT[q - 1], []).append(("tokens_out", tokens_out, q))
            if RELAY_AT[q - 1] >= 0:
                events.setdefault(RELAY_AT[q - 1], []).append(("tokens_relay", tokens_relay, q))
            events.setdefault(PAIR_AT[q - 1], []).append(("tokens_pair", tokens_pair, q))
            events.setdefault(UNITS * q - 1, []).append(("low_rank", low_rank, q))
        for q in range(CHUNKS - 1):
            done = UNITS * (q + 1) - 1 + SKEW[3]
            events.setdefault(done, []).append(("to_owning_core", to_owning_core, q))
            events.setdefault(done + AFTER[0], []).append(("to_owners", to_owners, q))
            events.setdefault(done + AFTER[1], []).append(("to_z", to_z, q))
        stages = [("first", 0, first), ("sum_1", SKEW[0], sum_1), ("sum_2", SKEW[1], sum_2)]
        stages += [("relay", SKEW[2], relay), ("second", SKEW[3], second)]
        steps = units + SKEW[3]
        late = [item for at, todo in sorted(events.items()) if at >= steps for item in todo]

        @pl.loop(0, (steps + UNITS - 1) // UNITS)
        def _(turn):
            for step in range(UNITS):
                for name, skew, stage in stages:
                    back, g = divmod(step - skew, UNITS)

                    @pl.when((turn + back >= 0) & (turn + back < CHUNKS))
                    def _():
                        scope(name, run, stage, turn + back, g)

                for at, todo in sorted(events.items()):
                    if at % UNITS != step or at >= steps:
                        continue

                    @pl.when(turn == at // UNITS)
                    def _():
                        for name, function, q in todo:
                            scope(name, function, q)

        last = CHUNKS - 1
        scope("to_owning_core", to_owning_core, last)
        for name, function, q in late:
            if q % 2 != last % 2:
                scope(name, function, q)
        scope("to_owners", to_owners, last)
        for name, function, q in late:
            if q % 2 == last % 2:
                scope(name, function, q)
        for q in range(CHUNKS):
            scope("finish", finish, q)

    vmem = pltpu.VMEM
    dma = pltpu.SemaphoreType.DMA
    scratch = [
        vmem((CHUNKS, rows, wide_k), BF16),
        vmem((UNITS - 1, wide_k, 2 * block), BF16),
        vmem((wide_k, block), BF16),
        vmem((columns, depth + LANE), BF16),
        vmem((units, rows, 2 * block), BF16),
        vmem((units, (ranks_x - 1) * 2 * own, 2 * block), BF16),
        vmem((units, (ranks_x - 1) * own, 2 * block), BF16),
        vmem((units, ranks_x * own, 2 * block), BF16),
        vmem((units, own, 2 * block), F32),
        vmem((units, rows, block), BF16),
        vmem((CHUNKS, rows, depth + LANE), F32),
        vmem((HALVES, rows, depth), BF16),
        vmem((HALVES, rows, depth), BF16),
        vmem((HALVES, rows, depth), BF16),
        vmem((HALVES, (ranks_y - 1) * 2 * part, depth), BF16),
        vmem((HALVES, part, depth), BF16),
        vmem((HALVES, part, depth), BF16),
        vmem((2, groups, columns), F32),
        vmem((blocks, depth), F32),
        vmem((2, depth, LANE), F32),
        vmem((2, LANE, columns), F32),
        vmem((columns, LANE), F32),
        vmem((LANE, depth), F32),
        vmem((depth, 2 * LANE), BF16),
        vmem((LANE, depth), BF16),
        dma((2, UNITS)),
        dma((blocks,)),
        dma((9,)),
        dma((HALVES,)), dma((chips - 1,)), dma((HALVES,)), dma((HALVES,)), dma((CHUNKS,)), dma((CHUNKS,)),
        dma((units,)), dma((units,)), dma((units,)), dma((units,)),
        dma((units,)), dma((units,)), dma((units,)),
        dma((HALVES,)), dma((HALVES,)), dma((HALVES,)), dma((HALVES,)),
        dma((HALVES,)), dma((HALVES,)),
    ]
    return kernel, scratch


def solution(mesh):
    n_wide, n_narrow = mesh.shape["wide"], mesh.shape["narrow"]

    def shards(tokens, gate_codes, up_codes, *rest):
        tok_rows = tokens.shape[0]
        depth, columns = gate_codes.shape
        kernel, scratch = make_kernel(n_wide, n_narrow, depth, columns, tok_rows)
        in_specs = [pl.BlockSpec(memory_space=pltpu.VMEM)] + [
            pl.BlockSpec(memory_space=pl.ANY)
        ] * 12
        return pl.pallas_call(
            kernel,
            out_shape=jax.ShapeDtypeStruct((tok_rows, depth), F32),
            in_specs=in_specs,
            out_specs=pl.BlockSpec(memory_space=pltpu.VMEM),
            scratch_shapes=scratch,
            compiler_params=pltpu.CompilerParams(
                collective_id=0, has_side_effects=True, vmem_limit_bytes=60 << 20
            ),
        )(tokens, gate_codes, up_codes, *rest)

    placed = (
        P("wide", "narrow"),
        P("narrow", "wide"),
        P("narrow", "wide"),
        P("narrow", "wide"),
        P("narrow", "wide"),
        P("wide", "narrow"),
        P("wide", "narrow"),
        P("narrow", None),
        P(None, "wide"),
        P("narrow", None),
        P(None, "wide"),
        P("wide", None),
        P(None, "narrow"),
    )
    return jax.shard_map(
        shards, mesh=mesh, in_specs=placed, out_specs=P("wide", "narrow"), check_vma=False
    )
```

```python
import jax
import jax.numpy as jnp
from jax import lax
from jax.experimental import pallas as pl
from jax.experimental.pallas import tpu as pltpu
from jax.sharding import PartitionSpec as P

MESH = pl.DeviceIdType.MESH
F32 = jnp.float32
BF16 = jnp.bfloat16
LANE = 128
HALVES = 2
CHUNKS = 4
UNITS = 7
X_FIRST = (1, 3, 5)
SKEW = (4, 8, 12, 16)
AFTER = (3, 9)
OUT_AT = (-1, 0, 3)
RELAY_AT = (-1, 4, 10)
PAIR_AT = (1, 9, 16)
PIECES = 2
FAR_FIRST = (2, 1, 3)
DIRECT = (4, 5, 6)
SPREAD = 3


def remote(src, dst, send_sem, recv_sem, device):
    return pltpu.make_async_remote_copy(
        src_ref=src,
        dst_ref=dst,
        send_sem=send_sem,
        recv_sem=recv_sem,
        device_id=device,
        device_id_type=MESH,
    )


def aligned(value, size):
    return pl.multiple_of(value, size)


def make_kernel(n_wide, n_narrow, depth, columns, tok_rows):
    chips = n_wide // 2
    ranks_y = chips // 2
    part = tok_rows // HALVES
    rows = chips * part
    ranks_x = n_narrow // 2
    own = rows // n_narrow
    groups = depth // LANE
    blocks = columns // LANE
    wide_k = depth + 2 * LANE
    block = 2 * LANE
    units = CHUNKS * UNITS
    last_block = (UNITS - 1) * block

    def kernel(
        tok, gate_codes, up_codes, gate_scale, up_scale, down_codes, down_scale,
        gate_left, gate_right, up_left, up_right, down_left, down_right,
        out,
        x_all, w_up, w_last, w_down, partial, land_1, land_2, half_sum, own_sum, hidden, acc,
        core_send, core_land, out_send, out_land, z_send, z_land,
        scale_v, dscale_v, left_v, right_v, dleft_v, dright_v, left_b, dright_b,
        load_w, load_d, load_s,
        tok_send, tok_first, tok_recv, tok_recv_z, pair_send, pair_recv,
        ss_1, rs_1, ss_2, rs_2, hid_send, hid_recv_1, hid_recv_2,
        core_ss, core_rs, out_ss, out_rs, z_ss, z_rs,
        piece_cs, piece_cr, piece_os, piece_or, piece_zs, piece_zr,
    ):
        w = lax.axis_index("wide")
        n = lax.axis_index("narrow")
        core, y, zl = lax.rem(w, 2), lax.rem(w // 2, ranks_y), w // chips
        x, zh = n // 2, lax.rem(n, 2)
        sibling = (w + 1 - 2 * core, n)
        z_peer = (w, x * 2 + (1 - zh))

        def y_peer(d):
            return lax.rem(y + d, ranks_y)

        def chip_at(yi, zi):
            return (zi * chips + yi * 2 + core, n)

        def tok_place(yi, zi, count=1):
            return pl.ds(aligned((yi * 2 + zi) * part, part), count * part)

        def x_peer(d):
            return lax.rem(x + d, ranks_x)

        small = [
            pltpu.make_async_copy(gate_left, left_v.at[0], load_s.at[0]),
            pltpu.make_async_copy(up_left, left_v.at[1], load_s.at[1]),
            pltpu.make_async_copy(gate_scale, scale_v.at[0], load_s.at[2]),
            pltpu.make_async_copy(up_scale, scale_v.at[1], load_s.at[3]),
            pltpu.make_async_copy(gate_right, right_v.at[0], load_s.at[4]),
            pltpu.make_async_copy(up_right, right_v.at[1], load_s.at[5]),
            pltpu.make_async_copy(down_scale, dscale_v, load_s.at[6]),
            pltpu.make_async_copy(down_left, dleft_v, load_s.at[7]),
            pltpu.make_async_copy(down_right, dright_v, load_s.at[8]),
        ]
        feats = pl.ds(0, depth)

        def cols_of(g, size=block):
            return pl.ds(aligned(g * block, size), size)

        def up_loads(g, target, size):
            return [
                pltpu.make_async_copy(
                    codes.at[:, cols_of(g, size)],
                    target.at[feats, pl.ds(i * size, size)],
                    load_w.at[i, g],
                )
                for i, codes in enumerate((gate_codes, up_codes))
            ]

        def down_load(g):
            here = pl.ds(aligned(g * LANE, LANE), LANE)
            return pltpu.make_async_copy(
                down_codes.at[here, :], w_down.at[here, feats], load_d.at[g]
            )

        with jax.named_scope("issue"):
            for copy in small[:6]:
                copy.start()

            @pl.loop(0, UNITS - 1)
            def _(g):
                for copy in up_loads(g, w_up.at[g], block):
                    copy.start()

            for copy in up_loads(UNITS - 1, w_last, LANE) + small[6:]:
                copy.start()

            @pl.loop(0, blocks)
            def _(g):
                down_load(g).start()

        with jax.named_scope("greet"):
            barrier = pltpu.get_barrier_semaphore()
            greet = [chip_at(y_peer(d), zi) for d in range(1, ranks_y) for zi in range(2)]
            greet += [chip_at(y, 1 - zl)]
            greet += [(w, x_peer(d) * 2 + zi) for d in range(1, ranks_x) for zi in range(2)]
            greet += [z_peer, sibling]
            for device in greet:
                pl.semaphore_signal(barrier, inc=1, device_id=device, device_id_type=MESH)
            pl.semaphore_wait(barrier, len(greet))

        place = tok_place(y, zl)

        def tokens_out(q):
            h, c = q // 2, q % 2

            @pl.when(core == c)
            def _():
                def send(recv, device):
                    remote(
                        tok.at[pl.ds(h * part, part), :],
                        x_all.at[q, place, feats],
                        tok_send.at[h],
                        recv,
                        device,
                    ).start()

                send(tok_first.at[0] if q == 0 else tok_recv_z.at[h], chip_at(y, 1 - zl))
                for d in range(1, ranks_y):
                    send(tok_first.at[d] if q == 0 else tok_recv.at[h], chip_at(y_peer(d), zl))
                    if q == 0:
                        send(tok_first.at[ranks_y - 1 + d], chip_at(y_peer(d), 1 - zl))
                x_all[q, place, feats] = tok[pl.ds(h * part, part), :]

        def tokens_got(q, count, recv):
            got = x_all.at[q, pl.ds(0, count * part), feats]
            return remote(got, got, tok_send.at[q // 2], recv.at[q // 2], sibling)

        def tokens_relay(q):
            @pl.when(core == q % 2)
            def _():
                tokens_got(q, 1, tok_recv_z).wait_recv()
                here = x_all.at[q, tok_place(y, 1 - zl), feats]
                for d in range(1, ranks_y):
                    remote(
                        here, here, tok_send.at[q // 2], tok_recv.at[q // 2], chip_at(y_peer(d), zl)
                    ).start()

        def pair_copy(q):
            both = x_all.at[q, :, feats]
            return remote(both, both, pair_send.at[q], pair_recv.at[q], sibling)

        def pass_on(at):
            here = x_all.at[0, at, feats]
            remote(here, here, pair_send.at[0], pair_recv.at[0], sibling).start()

        def tokens_pair(q):
            @pl.when(core == q % 2)
            def _():
                if q > 0:
                    tokens_got(q, chips - 2, tok_recv).wait_recv()
                    pair_copy(q).start()
                else:
                    pass_on(place)
                    for d in (0, 1, 3, 4, 6, 2, 5):
                        side = 0 if d == 0 else (d - 1) % (ranks_y - 1) + 1
                        yi = lax.rem(y + ranks_y - side, ranks_y)
                        here = tok_place(yi, zl if 0 < d < ranks_y else 1 - zl)
                        got = x_all.at[q, here, feats]
                        remote(got, got, tok_send.at[0], tok_first.at[d], sibling).wait_recv()
                        pass_on(here)
                tokens_got(q, chips - 1, tok_recv).wait_send()

        def low_rank(q):
            @pl.when(core != q % 2)
            def _():
                pair_copy(q).wait_recv()

            x_all[q, :, pl.ds(depth, 2 * LANE)] = jnp.dot(
                x_all[q, :, feats], left_b[...], preferred_element_type=F32
            ).astype(BF16)

        def prepare():
            for copy in small[:6]:
                copy.wait()
            left_b[:, pl.ds(0, LANE)] = left_v[0].astype(BF16)
            left_b[:, pl.ds(LANE, LANE)] = left_v[1].astype(BF16)

            def widen(g, target, size):
                for copy in up_loads(g, target, size):
                    copy.wait()
                for i in range(2):
                    here = pl.ds(i * size, size)
                    for k in range(groups):
                        at = pl.ds(k * LANE, LANE)
                        scale = scale_v[i, pl.ds(k, 1), cols_of(g, size)]
                        target[at, here] = (target[at, here].astype(F32) * scale).astype(BF16)
                    right = right_v[i, :, cols_of(g, size)].astype(BF16)
                    target[pl.ds(depth + i * LANE, LANE), here] = right
                    target[pl.ds(depth + (1 - i) * LANE, LANE), here] = jnp.zeros_like(right)

            @pl.loop(0, UNITS - 1)
            def _(g):
                widen(g, w_up.at[g], block)

            widen(UNITS - 1, w_last, LANE)
            for copy in small[6:]:
                copy.wait()
            dright_b[...] = dright_v[...].astype(BF16)

            @pl.loop(0, blocks)
            def _(g):
                down_load(g).wait()
                here = pl.ds(aligned(g * LANE, LANE), LANE)
                scale = dscale_v[pl.ds(g, 1), :]
                w_down[here, feats] = (w_down[here, feats].astype(F32) * scale).astype(BF16)
                w_down[here, pl.ds(depth, LANE)] = dleft_v[here, :].astype(BF16)

        def run(stage, q, g):
            stage(q * UNITS + g, q, g, g in X_FIRST, LANE if g == UNITS - 1 else block)

        def start_of(x_first, xi, zi):
            return aligned(xi * 2 * own + zi * own if x_first else zi * ranks_x * own + xi * own, own)

        def bytes_of(buffer, u, count, size, send, recv):
            at = buffer.at[u, pl.ds(0, count), pl.ds(0, size)]
            return remote(at, at, send.at[u], recv.at[u], sibling)

        def wait_1(u, x_first, size):
            count = (ranks_x - 1) * 2 * own if x_first else ranks_x * own
            return bytes_of(land_1, u, count, size, ss_1, rs_1)

        def wait_2(u, x_first, size):
            count = own if x_first else (ranks_x - 1) * own
            return bytes_of(land_2, u, count, size, ss_2, rs_2)

        def in_two_ways(q, g, straight, stepwise):
            if g not in DIRECT:
                stepwise()
                return
            pl.when(q == CHUNKS - 1)(straight)
            pl.when(q < CHUNKS - 1)(stepwise)

        def slots(u, x_first, cols):
            for d in range(ranks_x):
                for dz in range(2):
                    if d == 0 and dz == 0:
                        continue
                    if x_first:
                        one, at = d > 0, (d - 1) * 2 + dz if d > 0 else 0
                    else:
                        one, at = dz == 1, d if dz == 1 else d - 1
                    here = pl.ds(at * own, own)
                    yield d, dz, one, (land_1 if one else land_2).at[u, here, cols]

        def first(u, q, g, x_first, size):
            cols = pl.ds(0, 2 * size)
            weights = w_up[g] if size == block else w_last[...]
            partial[u, :, cols] = jnp.dot(
                x_all[q], weights, preferred_element_type=F32
            ).astype(BF16)
            def straight():
                for d, dz, one, land in slots(u, x_first, cols):
                    xi = x_peer(d)
                    zi = 1 - zh if dz else zh
                    remote(
                        partial.at[u, pl.ds(start_of(x_first, xi, zi), own), cols],
                        land,
                        (ss_1 if one else ss_2).at[u],
                        (rs_1 if one else rs_2).at[u],
                        (w, xi * 2 + zi),
                    ).start()

            def stepwise():
                if x_first:
                    for d in range(1, ranks_x):
                        xi = x_peer(d)
                        remote(
                            partial.at[u, pl.ds(start_of(True, xi, 0), 2 * own), cols],
                            land_1.at[u, pl.ds((d - 1) * 2 * own, 2 * own), cols],
                            ss_1.at[u],
                            rs_1.at[u],
                            (w, xi * 2 + zh),
                        ).start()
                else:
                    remote(
                        partial.at[u, pl.ds(start_of(False, 0, 1 - zh), ranks_x * own), cols],
                        land_1.at[u, pl.ds(0, ranks_x * own), cols],
                        ss_1.at[u],
                        rs_1.at[u],
                        z_peer,
                    ).start()

            in_two_ways(q, g, straight, stepwise)

        def hidden_copy(u, at, size, recv, device):
            here = hidden.at[u, at, pl.ds(0, size)]
            return remote(here, here, hid_send.at[u], recv.at[u], device)

        def activate(u, q, total, x_first, size):
            gate, up = total[:, :size], total[:, size:]
            mine = pl.ds(start_of(x_first, x, zh), own)
            hidden[u, mine, pl.ds(0, size)] = (gate / (1.0 + jnp.exp(-gate)) * up).astype(BF16)
            along_z = hid_recv_1 if x_first else hid_recv_2
            along_x = hid_recv_2 if x_first else hid_recv_1
            hidden_copy(u, mine, size, along_z, z_peer).start()
            for d in range(1, ranks_x):
                xi = x_peer(d) * 2
                hidden_copy(u, mine, size, along_x, (w, xi + zh)).start()

            @pl.when(q >= SPREAD)
            def _():
                for d in range(1, ranks_x):
                    device = (w, x_peer(d) * 2 + 1 - zh)
                    hidden_copy(u, mine, size, hid_recv_2, device).start()

        def sum_1(u, q, g, x_first, size):
            cols = pl.ds(0, 2 * size)
            wait_1(u, x_first, 2 * size).wait_recv()

            def straight():
                wait_2(u, x_first, 2 * size).wait_recv()
                total = partial[u, pl.ds(start_of(x_first, x, zh), own), cols].astype(F32)
                for _, _, _, land in slots(u, x_first, cols):
                    total = total + land[...].astype(F32)
                activate(u, q, total, x_first, size)

            def stepwise():
                if x_first:

                    def total(zi):
                        value = partial[u, pl.ds(start_of(True, x, zi), own), cols].astype(F32)
                        for d in range(ranks_x - 1):
                            at = pl.ds(aligned(d * 2 * own + zi * own, own), own)
                            value = value + land_1[u, at, cols].astype(F32)
                        return value

                    half_sum[u, pl.ds(0, own), cols] = total(1 - zh).astype(BF16)
                    remote(
                        half_sum.at[u, pl.ds(0, own), cols],
                        land_2.at[u, pl.ds(0, own), cols],
                        ss_2.at[u],
                        rs_2.at[u],
                        z_peer,
                    ).start()
                    own_sum[u, :, cols] = total(zh)
                else:
                    group = pl.ds(start_of(False, 0, zh), ranks_x * own)
                    got = pl.ds(0, ranks_x * own)
                    half_sum[u, got, cols] = (
                        partial[u, group, cols].astype(F32) + land_1[u, got, cols].astype(F32)
                    ).astype(BF16)
                    for d in range(1, ranks_x):
                        xi = x_peer(d)
                        remote(
                            half_sum.at[u, pl.ds(aligned(xi * own, own), own), cols],
                            land_2.at[u, pl.ds((d - 1) * own, own), cols],
                            ss_2.at[u],
                            rs_2.at[u],
                            (w, xi * 2 + zh),
                        ).start()
                    mine = pl.ds(aligned(x * own, own), own)
                    own_sum[u, :, cols] = (
                        partial[u, pl.ds(start_of(False, x, zh), own), cols].astype(F32)
                        + land_1[u, mine, cols].astype(F32)
                    )

            in_two_ways(q, g, straight, stepwise)

        def sum_2(u, q, g, x_first, size):
            def stepwise():
                wait_2(u, x_first, 2 * size).wait_recv()
                total = own_sum[u, :, pl.ds(0, 2 * size)]
                for d in range(1 if x_first else ranks_x - 1):
                    total = total + land_2[u, pl.ds(d * own, own), pl.ds(0, 2 * size)].astype(F32)
                activate(u, q, total, x_first, size)

            in_two_ways(q, g, lambda: None, stepwise)

        def wait_early(u, x_first, size):
            count = own if x_first else (ranks_x - 1) * own
            return bytes_of(hidden, u, count, size, hid_send, hid_recv_1)

        def wait_late(u, x_first, size):
            count = (ranks_x - 1) * 2 * own if x_first else ranks_x * own
            return bytes_of(hidden, u, count, size, hid_send, hid_recv_2)

        def relay(u, q, g, x_first, size):
            wait_early(u, x_first, size).wait_recv()

            @pl.when(q < SPREAD)
            def _():
                for d in range(1, ranks_x):
                    xi = x_peer(d)
                    if x_first:
                        at = pl.ds(start_of(True, x, 1 - zh), own)
                        device = (w, xi * 2 + zh)
                    else:
                        at = pl.ds(start_of(False, xi, zh), own)
                        device = z_peer
                    hidden_copy(u, at, size, hid_recv_2, device).start()

        def second(u, q, g, x_first, size):
            wait_late(u, x_first, size).wait_recv()
            acc[q] += jnp.dot(
                hidden[u, :, pl.ds(0, size)],
                w_down[cols_of(g, size), :],
                preferred_element_type=F32,
            )
            wait_1(u, x_first, 2 * size).wait_send()
            wait_2(u, x_first, 2 * size).wait_send()
            bytes_of(hidden, u, (n_narrow - 1) * own, size, hid_send, hid_recv_2).wait_send()

        def core_copy(h):
            return remote(core_send.at[h], core_land.at[h], core_ss.at[h], core_rs.at[h], sibling)

        def to_owning_core(q):
            low = acc[q, :, pl.ds(depth, LANE)].astype(BF16)
            acc[q, :, feats] += jnp.dot(low, dright_b[...], preferred_element_type=F32)

            @pl.when(core != q % 2)
            def _():
                core_send[q // 2] = acc[q, :, feats].astype(BF16)
                core_copy(q // 2).start()

        def to_owners(q):
            h = q // 2

            @pl.when(core == q % 2)
            def _():
                core_copy(h).wait_recv()
                both = acc[q, :, feats] + core_land[h].astype(F32)
                acc[q, :, feats] = both
                out_send[h] = both.astype(BF16)
                for d in range(1, ranks_y):
                    yi = y_peer(d)
                    at = pl.ds((d - 1) * 2 * part, 2 * part)
                    remote(
                        out_send.at[h, tok_place(yi, 0, 2)],
                        out_land.at[h, at],
                        out_ss.at[h],
                        out_rs.at[h],
                        chip_at(yi, zl),
                    ).start()

        def out_wait(h):
            got = out_land.at[h]
            return remote(got, got, out_ss.at[h], out_rs.at[h], sibling)

        def z_copy(h):
            return remote(z_send.at[h], z_land.at[h], z_ss.at[h], z_rs.at[h], chip_at(y, 1 - zl))

        def to_z(q):
            h = q // 2

            @pl.when(core == q % 2)
            def _():
                out_wait(h).wait()

                def total(zi):
                    value = acc[q, tok_place(y, zi), feats]
                    for d in range(ranks_y - 1):
                        at = pl.ds(aligned((d * 2 + zi) * part, part), part)
                        value = value + out_land[h, at].astype(F32)
                    return value

                z_send[h] = total(1 - zl).astype(BF16)
                z_copy(h).start()
                acc[q, place, feats] = total(zl)

        def finish(q):
            h = q // 2

            @pl.when(core == q % 2)
            def _():
                total = acc[q, place, feats]
                z_copy(h).wait()
                out[pl.ds(h * part, part), :] = total + z_land[h].astype(F32)
                pair_copy(q).wait_send()

            @pl.when(core != q % 2)
            def _():
                core_copy(h).wait_send()

        last = CHUNKS - 1
        last_h = last // 2
        piece = depth // PIECES

        def piece_copy(i):
            at = pl.ds(i * piece, piece)
            return remote(
                core_send.at[last_h, :, at],
                core_land.at[last_h, :, at],
                piece_cs.at[i],
                piece_cr.at[i],
                sibling,
            )

        def piece_wait(i):
            got = out_land.at[last_h, pl.ds(0, (chips - 2) * part), pl.ds(i * piece, piece)]
            rest = z_land.at[last_h, :, pl.ds(i * piece, piece)]
            return [
                remote(got, got, piece_os.at[i], piece_or.at[i], sibling),
                remote(rest, rest, piece_zs.at[i], piece_zr.at[i], sibling),
            ]

        def last_to_core():
            low = acc[last, :, pl.ds(depth, LANE)].astype(BF16)
            for i in range(PIECES):
                at = pl.ds(i * piece, piece)
                acc[last, :, at] += jnp.dot(low, dright_b[:, at], preferred_element_type=F32)

                @pl.when(core != last % 2)
                def _():
                    core_send[last_h, :, at] = acc[last, :, at].astype(BF16)
                    piece_copy(i).start()

        def last_to_owners():
            @pl.when(core == last % 2)
            def _():
                for i in range(PIECES):
                    at = pl.ds(i * piece, piece)
                    piece_copy(i).wait_recv()
                    both = acc[last, :, at] + core_land[last_h, :, at].astype(F32)
                    acc[last, :, at] = both
                    out_send[last_h, :, at] = both.astype(BF16)

                    def send(yi, zi, land, out_s=piece_os, out_r=piece_or):
                        remote(
                            out_send.at[last_h, tok_place(yi, zi), at],
                            land,
                            out_s.at[i],
                            out_r.at[i],
                            chip_at(yi, zi),
                        ).start()

                    for d in FAR_FIRST:
                        here = pl.ds(aligned(((d - 1) * 2 + zl) * part, part), part)
                        for zi in range(2):
                            send(y_peer(d), zi, out_land.at[last_h, here, at])
                    send(y, 1 - zl, z_land.at[last_h, :, at], piece_zs, piece_zr)

        def last_finish():
            @pl.when(core == last % 2)
            def _():
                for i in range(PIECES):
                    at = pl.ds(i * piece, piece)
                    for copy in piece_wait(i):
                        copy.wait()
                    total = acc[last, place, at] + z_land[last_h, :, at].astype(F32)
                    for d in range(chips - 2):
                        total = total + out_land[last_h, pl.ds(d * part, part), at].astype(F32)
                    out[pl.ds(last_h * part, part), at] = total
                pair_copy(last).wait_send()

            @pl.when(core != last % 2)
            def _():
                for i in range(PIECES):
                    piece_copy(i).wait_send()

        def scope(name, function, *given):
            with jax.named_scope(name):
                function(*given)

        scope("tokens_out", tokens_out, 0)
        acc[...] = jnp.zeros_like(acc)
        scope("prepare", prepare)
        if OUT_AT[0] < 0:
            scope("tokens_out", tokens_out, 1)
        scope("tokens_pair", tokens_pair, 0)
        if RELAY_AT[0] < 0:
            scope("tokens_relay", tokens_relay, 1)
        scope("low_rank", low_rank, 0)

        events = {}
        for q in range(1, CHUNKS):
            if OUT_AT[q - 1] >= 0:
                events.setdefault(OUT_AT[q - 1], []).append(("tokens_out", tokens_out, q))
            if RELAY_AT[q - 1] >= 0:
                events.setdefault(RELAY_AT[q - 1], []).append(("tokens_relay", tokens_relay, q))
            events.setdefault(PAIR_AT[q - 1], []).append(("tokens_pair", tokens_pair, q))
            events.setdefault(UNITS * q - 1, []).append(("low_rank", low_rank, q))
        for q in range(CHUNKS - 1):
            done = UNITS * (q + 1) - 1 + SKEW[3]
            events.setdefault(done, []).append(("to_owning_core", to_owning_core, q))
            events.setdefault(done + AFTER[0], []).append(("to_owners", to_owners, q))
            events.setdefault(done + AFTER[1], []).append(("to_z", to_z, q))
        stages = [("first", 0, first), ("sum_1", SKEW[0], sum_1), ("sum_2", SKEW[1], sum_2)]
        stages += [("relay", SKEW[2], relay), ("second", SKEW[3], second)]
        steps = units + SKEW[3]
        late = [item for at, todo in sorted(events.items()) if at >= steps for item in todo]

        @pl.loop(0, (steps + UNITS - 1) // UNITS)
        def _(turn):
            for step in range(UNITS):
                for name, skew, stage in stages:
                    back, g = divmod(step - skew, UNITS)

                    @pl.when((turn + back >= 0) & (turn + back < CHUNKS))
                    def _():
                        scope(name, run, stage, turn + back, g)

                for at, todo in sorted(events.items()):
                    if at % UNITS != step or at >= steps:
                        continue

                    @pl.when(turn == at // UNITS)
                    def _():
                        for name, function, q in todo:
                            scope(name, function, q)

        scope("to_owning_core", last_to_core)
        for name, function, q in late:
            if q % 2 != last % 2:
                scope(name, function, q)
        scope("to_owners", last_to_owners)
        for name, function, q in late:
            if q % 2 == last % 2:
                scope(name, function, q)
        for q in range(CHUNKS - 1):
            scope("finish", finish, q)
        scope("finish_last", last_finish)

    vmem = pltpu.VMEM
    dma = pltpu.SemaphoreType.DMA
    scratch = [
        vmem((CHUNKS, rows, wide_k), BF16),
        vmem((UNITS - 1, wide_k, 2 * block), BF16),
        vmem((wide_k, block), BF16),
        vmem((columns, depth + LANE), BF16),
        vmem((units, rows, 2 * block), BF16),
        vmem((units, (ranks_x - 1) * 2 * own, 2 * block), BF16),
        vmem((units, (ranks_x - 1) * own, 2 * block), BF16),
        vmem((units, ranks_x * own, 2 * block), BF16),
        vmem((units, own, 2 * block), F32),
        vmem((units, rows, block), BF16),
        vmem((CHUNKS, rows, depth + LANE), F32),
        vmem((HALVES, rows, depth), BF16),
        vmem((HALVES, rows, depth), BF16),
        vmem((HALVES, rows, depth), BF16),
        vmem((HALVES, (ranks_y - 1) * 2 * part, depth), BF16),
        vmem((HALVES, part, depth), BF16),
        vmem((HALVES, part, depth), BF16),
        vmem((2, groups, columns), F32),
        vmem((blocks, depth), F32),
        vmem((2, depth, LANE), F32),
        vmem((2, LANE, columns), F32),
        vmem((columns, LANE), F32),
        vmem((LANE, depth), F32),
        vmem((depth, 2 * LANE), BF16),
        vmem((LANE, depth), BF16),
        dma((2, UNITS)),
        dma((blocks,)),
        dma((9,)),
        dma((HALVES,)), dma((chips - 1,)), dma((HALVES,)), dma((HALVES,)), dma((CHUNKS,)), dma((CHUNKS,)),
        dma((units,)), dma((units,)), dma((units,)), dma((units,)),
        dma((units,)), dma((units,)), dma((units,)),
        dma((HALVES,)), dma((HALVES,)), dma((HALVES,)), dma((HALVES,)),
        dma((HALVES,)), dma((HALVES,)),
        dma((PIECES,)), dma((PIECES,)), dma((PIECES,)), dma((PIECES,)),
        dma((PIECES,)), dma((PIECES,)),
    ]
    return kernel, scratch


def solution(mesh):
    n_wide, n_narrow = mesh.shape["wide"], mesh.shape["narrow"]

    def shards(tokens, gate_codes, up_codes, *rest):
        tok_rows = tokens.shape[0]
        depth, columns = gate_codes.shape
        kernel, scratch = make_kernel(n_wide, n_narrow, depth, columns, tok_rows)
        in_specs = [pl.BlockSpec(memory_space=pltpu.VMEM)] + [
            pl.BlockSpec(memory_space=pl.ANY)
        ] * 12
        return pl.pallas_call(
            kernel,
            out_shape=jax.ShapeDtypeStruct((tok_rows, depth), F32),
            in_specs=in_specs,
            out_specs=pl.BlockSpec(memory_space=pltpu.VMEM),
            scratch_shapes=scratch,
            compiler_params=pltpu.CompilerParams(
                collective_id=0, has_side_effects=True, vmem_limit_bytes=60 << 20
            ),
        )(tokens, gate_codes, up_codes, *rest)

    placed = (
        P("wide", "narrow"),
        P("narrow", "wide"),
        P("narrow", "wide"),
        P("narrow", "wide"),
        P("narrow", "wide"),
        P("wide", "narrow"),
        P("wide", "narrow"),
        P("narrow", None),
        P(None, "wide"),
        P("narrow", None),
        P(None, "wide"),
        P("wide", None),
        P(None, "narrow"),
    )
    return jax.shard_map(
        shards, mesh=mesh, in_specs=placed, out_specs=P("wide", "narrow"), check_vma=False
    )
```

```python
import jax
import jax.numpy as jnp
from jax import lax
from jax.experimental import pallas as pl
from jax.experimental.pallas import tpu as pltpu
from jax.sharding import PartitionSpec as P

MESH = pl.DeviceIdType.MESH
F32 = jnp.float32
BF16 = jnp.bfloat16
LANE = 128
HALVES = 2
CHUNKS = 4
UNITS = 7
X_FIRST = (1, 3, 5)
SKEW = (4, 8, 12, 16)
AFTER = (3, 9)
OUT_AT = (-1, 0, 3)
RELAY_AT = (-1, 4, 10)
PAIR_AT = (3, 9, 16)
WINDOW = 14
SPREAD = 3


def remote(src, dst, send_sem, recv_sem, device):
    return pltpu.make_async_remote_copy(
        src_ref=src,
        dst_ref=dst,
        send_sem=send_sem,
        recv_sem=recv_sem,
        device_id=device,
        device_id_type=MESH,
    )


def aligned(value, size):
    return pl.multiple_of(value, size)


def make_kernel(n_wide, n_narrow, depth, columns, tok_rows):
    chips = n_wide // 2
    ranks_y = chips // 2
    part = tok_rows // HALVES
    rows = chips * part
    ranks_x = n_narrow // 2
    own = rows // n_narrow
    groups = depth // LANE
    blocks = columns // LANE
    wide_k = depth + 2 * LANE
    block = 2 * LANE
    units = CHUNKS * UNITS
    last_block = (UNITS - 1) * block

    def kernel(
        tok, gate_codes, up_codes, gate_scale, up_scale, down_codes, down_scale,
        gate_left, gate_right, up_left, up_right, down_left, down_right,
        out,
        x_all, w_up, w_last, w_down, partial, land_1, land_2, half_sum, own_sum, hidden, acc,
        core_send, core_land, out_send, out_land, z_send, z_land,
        scale_v, dscale_v, left_v, right_v, dleft_v, dright_v, left_b, dright_b,
        load_w, load_d, load_s,
        tok_send, tok_first, tok_recv, tok_recv_z, pair_send, pair_recv,
        unit_send, rs_1, rs_2, hid_recv_1, hid_recv_2,
        core_ss, core_rs, out_ss, out_rs, z_ss, z_rs,
    ):
        w = lax.axis_index("wide")
        n = lax.axis_index("narrow")
        core, y, zl = lax.rem(w, 2), lax.rem(w // 2, ranks_y), w // chips
        x, zh = n // 2, lax.rem(n, 2)
        sibling = (w + 1 - 2 * core, n)
        z_peer = (w, x * 2 + (1 - zh))

        def y_peer(d):
            return lax.rem(y + d, ranks_y)

        def chip_at(yi, zi):
            return (zi * chips + yi * 2 + core, n)

        def tok_place(yi, zi, count=1):
            return pl.ds(aligned((yi * 2 + zi) * part, part), count * part)

        def x_peer(d):
            return lax.rem(x + d, ranks_x)

        small = [
            pltpu.make_async_copy(gate_left, left_v.at[0], load_s.at[0]),
            pltpu.make_async_copy(up_left, left_v.at[1], load_s.at[1]),
            pltpu.make_async_copy(gate_scale, scale_v.at[0], load_s.at[2]),
            pltpu.make_async_copy(up_scale, scale_v.at[1], load_s.at[3]),
            pltpu.make_async_copy(gate_right, right_v.at[0], load_s.at[4]),
            pltpu.make_async_copy(up_right, right_v.at[1], load_s.at[5]),
            pltpu.make_async_copy(down_scale, dscale_v, load_s.at[6]),
            pltpu.make_async_copy(down_left, dleft_v, load_s.at[7]),
            pltpu.make_async_copy(down_right, dright_v, load_s.at[8]),
        ]
        feats = pl.ds(0, depth)

        def cols_of(g, size=block):
            return pl.ds(aligned(g * block, size), size)

        def up_loads(g, target, size):
            return [
                pltpu.make_async_copy(
                    codes.at[:, cols_of(g, size)],
                    target.at[feats, pl.ds(i * size, size)],
                    load_w.at[g],
                )
                for i, codes in enumerate((gate_codes, up_codes))
            ]

        def down_load(g):
            here = pl.ds(aligned(g * LANE, LANE), LANE)
            return pltpu.make_async_copy(
                down_codes.at[here, :], w_down.at[here, feats], load_d.at[0]
            )

        with jax.named_scope("issue"):
            for copy in small[:6]:
                copy.start()

            @pl.loop(0, UNITS - 1)
            def _(g):
                for copy in up_loads(g, w_up.at[g], block):
                    copy.start()

            for copy in up_loads(UNITS - 1, w_last, LANE) + small[6:]:
                copy.start()

            @pl.loop(0, blocks)
            def _(g):
                down_load(g).start()

        with jax.named_scope("greet"):
            barrier = pltpu.get_barrier_semaphore()
            greet = [chip_at(y_peer(d), zi) for d in range(1, ranks_y) for zi in range(2)]
            greet += [chip_at(y, 1 - zl)]
            greet += [(w, x_peer(d) * 2 + zi) for d in range(1, ranks_x) for zi in range(2)]
            greet += [z_peer, sibling]
            for device in greet:
                pl.semaphore_signal(barrier, inc=1, device_id=device, device_id_type=MESH)
            pl.semaphore_wait(barrier, len(greet))

        place = tok_place(y, zl)

        def tokens_out(q):
            h, c = q // 2, q % 2

            @pl.when(core == c)
            def _():
                def send(recv, device):
                    remote(
                        tok.at[pl.ds(h * part, part), :],
                        x_all.at[q, place, feats],
                        tok_send.at[h],
                        recv,
                        device,
                    ).start()

                send(tok_first.at[0] if q == 0 else tok_recv_z.at[h], chip_at(y, 1 - zl))
                for d in range(1, ranks_y):
                    send(tok_first.at[d] if q == 0 else tok_recv.at[h], chip_at(y_peer(d), zl))
                    if q == 0:
                        send(tok_first.at[ranks_y - 1 + d], chip_at(y_peer(d), 1 - zl))
                x_all[q, place, feats] = tok[pl.ds(h * part, part), :]

        def tokens_got(q, count, recv):
            got = x_all.at[q, pl.ds(0, count * part), feats]
            return remote(got, got, tok_send.at[q // 2], recv.at[q // 2], sibling)

        def tokens_relay(q):
            @pl.when(core == q % 2)
            def _():
                tokens_got(q, 1, tok_recv_z).wait_recv()
                here = x_all.at[q, tok_place(y, 1 - zl), feats]
                for d in range(1, ranks_y):
                    remote(
                        here, here, tok_send.at[q // 2], tok_recv.at[q // 2], chip_at(y_peer(d), zl)
                    ).start()

        def pair_copy(q):
            both = x_all.at[q, :, feats]
            return remote(both, both, pair_send.at[q], pair_recv.at[q], sibling)

        def pass_on(at):
            here = x_all.at[0, at, feats]
            remote(here, here, pair_send.at[0], pair_recv.at[0], sibling).start()

        def tokens_pair(q):
            @pl.when(core == q % 2)
            def _():
                if q > 0:
                    tokens_got(q, chips - 2, tok_recv).wait_recv()
                    pair_copy(q).start()
                else:
                    pass_on(place)
                    for d in (0, 1, 3, 4, 6, 2, 5):
                        side = 0 if d == 0 else (d - 1) % (ranks_y - 1) + 1
                        yi = lax.rem(y + ranks_y - side, ranks_y)
                        here = tok_place(yi, zl if 0 < d < ranks_y else 1 - zl)
                        got = x_all.at[q, here, feats]
                        remote(got, got, tok_send.at[0], tok_first.at[d], sibling).wait_recv()
                        pass_on(here)
                tokens_got(q, chips - 1, tok_recv).wait_send()

        def low_rank(q):
            @pl.when(core != q % 2)
            def _():
                pair_copy(q).wait_recv()

            x_all[q, :, pl.ds(depth, 2 * LANE)] = jnp.dot(
                x_all[q, :, feats], left_b[...], preferred_element_type=F32
            ).astype(BF16)

        def prepare():
            for copy in small[:6]:
                copy.wait()
            left_b[:, pl.ds(0, LANE)] = left_v[0].astype(BF16)
            left_b[:, pl.ds(LANE, LANE)] = left_v[1].astype(BF16)

            def widen(g, target, size):
                whole = target.at[feats, :]
                pltpu.make_async_copy(whole, whole, load_w.at[g]).wait()
                for i in range(2):
                    here = pl.ds(i * size, size)
                    for k in range(groups):
                        at = pl.ds(k * LANE, LANE)
                        scale = scale_v[i, pl.ds(k, 1), cols_of(g, size)]
                        target[at, here] = (target[at, here].astype(F32) * scale).astype(BF16)
                    right = right_v[i, :, cols_of(g, size)].astype(BF16)
                    target[pl.ds(depth + i * LANE, LANE), here] = right
                    target[pl.ds(depth + (1 - i) * LANE, LANE), here] = jnp.zeros_like(right)

            @pl.loop(0, UNITS - 1)
            def _(g):
                widen(g, w_up.at[g], block)

            widen(UNITS - 1, w_last, LANE)
            for copy in small[6:]:
                copy.wait()
            dright_b[...] = dright_v[...].astype(BF16)
            whole = w_down.at[:, feats]
            pltpu.make_async_copy(whole, whole, load_d.at[0]).wait()

            @pl.loop(0, blocks)
            def _(g):
                here = pl.ds(aligned(g * LANE, LANE), LANE)
                scale = dscale_v[pl.ds(g, 1), :]
                w_down[here, feats] = (w_down[here, feats].astype(F32) * scale).astype(BF16)
                w_down[here, pl.ds(depth, LANE)] = dleft_v[here, :].astype(BF16)

        def run(stage, q, g):
            stage(q * UNITS + g, q, g, g in X_FIRST, LANE if g == UNITS - 1 else block)

        def start_of(x_first, xi, zi):
            return aligned(xi * 2 * own + zi * own if x_first else zi * ranks_x * own + xi * own, own)

        def slot(u):
            return u - jnp.where(u >= WINDOW, WINDOW, 0)

        def arrival(recv, u):
            return recv.at[u if recv is hid_recv_2 else slot(u)]

        def bytes_of(buffer, u, count, size, recv):
            at = buffer.at[u, pl.ds(0, count), pl.ds(0, size)]
            return remote(at, at, unit_send.at[u], arrival(recv, u), sibling)

        def wait_1(u, x_first, size):
            count = (ranks_x - 1) * 2 * own if x_first else ranks_x * own
            return bytes_of(land_1, u, count, size, rs_1)

        def wait_2(u, x_first, size):
            count = own if x_first else (ranks_x - 1) * own
            return bytes_of(land_2, u, count, size, rs_2)

        def first(u, q, g, x_first, size):
            cols = pl.ds(0, 2 * size)
            weights = w_up[g] if size == block else w_last[...]
            partial[u, :, cols] = jnp.dot(
                x_all[q], weights, preferred_element_type=F32
            ).astype(BF16)
            if x_first:
                for d in range(1, ranks_x):
                    xi = x_peer(d)
                    remote(
                        partial.at[u, pl.ds(start_of(True, xi, 0), 2 * own), cols],
                        land_1.at[u, pl.ds((d - 1) * 2 * own, 2 * own), cols],
                        unit_send.at[u],
                        rs_1.at[slot(u)],
                        (w, xi * 2 + zh),
                    ).start()
            else:
                remote(
                    partial.at[u, pl.ds(start_of(False, 0, 1 - zh), ranks_x * own), cols],
                    land_1.at[u, pl.ds(0, ranks_x * own), cols],
                    unit_send.at[u],
                    rs_1.at[slot(u)],
                    z_peer,
                ).start()

        def hidden_copy(u, at, size, recv, device):
            here = hidden.at[u, at, pl.ds(0, size)]
            return remote(here, here, unit_send.at[u], arrival(recv, u), device)

        def activate(u, q, total, x_first, size):
            gate, up = total[:, :size], total[:, size:]
            mine = pl.ds(start_of(x_first, x, zh), own)
            hidden[u, mine, pl.ds(0, size)] = (gate / (1.0 + jnp.exp(-gate)) * up).astype(BF16)
            along_z = hid_recv_1 if x_first else hid_recv_2
            along_x = hid_recv_2 if x_first else hid_recv_1
            hidden_copy(u, mine, size, along_z, z_peer).start()
            for d in range(1, ranks_x):
                xi = x_peer(d) * 2
                hidden_copy(u, mine, size, along_x, (w, xi + zh)).start()

            @pl.when(q >= SPREAD)
            def _():
                for d in range(1, ranks_x):
                    device = (w, x_peer(d) * 2 + 1 - zh)
                    hidden_copy(u, mine, size, hid_recv_2, device).start()

        def sum_1(u, q, g, x_first, size):
            cols = pl.ds(0, 2 * size)
            wait_1(u, x_first, 2 * size).wait_recv()
            if x_first:

                def total(zi):
                    value = partial[u, pl.ds(start_of(True, x, zi), own), cols].astype(F32)
                    for d in range(ranks_x - 1):
                        at = pl.ds(aligned(d * 2 * own + zi * own, own), own)
                        value = value + land_1[u, at, cols].astype(F32)
                    return value

                half_sum[u, pl.ds(0, own), cols] = total(1 - zh).astype(BF16)
                remote(
                    half_sum.at[u, pl.ds(0, own), cols],
                    land_2.at[u, pl.ds(0, own), cols],
                    unit_send.at[u],
                    rs_2.at[slot(u)],
                    z_peer,
                ).start()
                own_sum[u, :, cols] = total(zh)
            else:
                group = pl.ds(start_of(False, 0, zh), ranks_x * own)
                got = pl.ds(0, ranks_x * own)
                half_sum[u, got, cols] = (
                    partial[u, group, cols].astype(F32) + land_1[u, got, cols].astype(F32)
                ).astype(BF16)
                for d in range(1, ranks_x):
                    xi = x_peer(d)
                    remote(
                        half_sum.at[u, pl.ds(aligned(xi * own, own), own), cols],
                        land_2.at[u, pl.ds((d - 1) * own, own), cols],
                        unit_send.at[u],
                        rs_2.at[slot(u)],
                        (w, xi * 2 + zh),
                    ).start()
                mine = pl.ds(aligned(x * own, own), own)
                own_sum[u, :, cols] = (
                    partial[u, pl.ds(start_of(False, x, zh), own), cols].astype(F32)
                    + land_1[u, mine, cols].astype(F32)
                )

        def sum_2(u, q, g, x_first, size):
            wait_2(u, x_first, 2 * size).wait_recv()
            total = own_sum[u, :, pl.ds(0, 2 * size)]
            for d in range(1 if x_first else ranks_x - 1):
                total = total + land_2[u, pl.ds(d * own, own), pl.ds(0, 2 * size)].astype(F32)
            activate(u, q, total, x_first, size)

        def wait_early(u, x_first, size):
            count = own if x_first else (ranks_x - 1) * own
            return bytes_of(hidden, u, count, size, hid_recv_1)

        def wait_late(u, x_first, size):
            count = (ranks_x - 1) * 2 * own if x_first else ranks_x * own
            return bytes_of(hidden, u, count, size, hid_recv_2)

        def relay(u, q, g, x_first, size):
            wait_early(u, x_first, size).wait_recv()

            @pl.when(q < SPREAD)
            def _():
                for d in range(1, ranks_x):
                    xi = x_peer(d)
                    if x_first:
                        at = pl.ds(start_of(True, x, 1 - zh), own)
                        device = (w, xi * 2 + zh)
                    else:
                        at = pl.ds(start_of(False, xi, zh), own)
                        device = z_peer
                    hidden_copy(u, at, size, hid_recv_2, device).start()

        def second(u, q, g, x_first, size):
            wait_late(u, x_first, size).wait_recv()
            acc[q] += jnp.dot(
                hidden[u, :, pl.ds(0, size)],
                w_down[cols_of(g, size), :],
                preferred_element_type=F32,
            )
            sent = w_down.at[pl.ds(0, (n_narrow - 1) * own * 3), pl.ds(0, size)]
            remote(sent, sent, unit_send.at[u], hid_recv_2.at[u], sibling).wait_send()

        def core_copy(h):
            return remote(core_send.at[h], core_land.at[h], core_ss.at[h], core_rs.at[h], sibling)

        def to_owning_core(q):
            low = acc[q, :, pl.ds(depth, LANE)].astype(BF16)
            acc[q, :, feats] += jnp.dot(low, dright_b[...], preferred_element_type=F32)

            @pl.when(core != q % 2)
            def _():
                core_send[q // 2] = acc[q, :, feats].astype(BF16)
                core_copy(q // 2).start()

        def out_copy(h, src, dst, send, recv, device):
            return remote(src, dst, send.at[h], recv.at[h], device)

        def to_owners(q):
            h = q // 2

            @pl.when(core == q % 2)
            def _():
                core_copy(h).wait_recv()
                both = acc[q, :, feats] + core_land[h].astype(F32)
                acc[q, :, feats] = both
                out_send[h] = both.astype(BF16)
                for d in range(1, ranks_y):
                    yi = y_peer(d)
                    if q < CHUNKS - 1:
                        at = pl.ds((d - 1) * 2 * part, 2 * part)
                        remote(
                            out_send.at[h, tok_place(yi, 0, 2)],
                            out_land.at[h, at],
                            out_ss.at[h],
                            out_rs.at[h],
                            chip_at(yi, zl),
                        ).start()
                        continue
                    for zi in range(2):
                        at = pl.ds(aligned(((d - 1) * 2 + zl) * part, part), part)
                        remote(
                            out_send.at[h, tok_place(yi, zi)],
                            out_land.at[h, at],
                            out_ss.at[h],
                            out_rs.at[h],
                            chip_at(yi, zi),
                        ).start()
                if q == CHUNKS - 1:
                    remote(
                        out_send.at[h, tok_place(y, 1 - zl)],
                        z_land.at[h],
                        z_ss.at[h],
                        z_rs.at[h],
                        chip_at(y, 1 - zl),
                    ).start()

        def out_wait(h):
            got = out_land.at[h]
            return remote(got, got, out_ss.at[h], out_rs.at[h], sibling)

        def z_copy(h):
            return remote(z_send.at[h], z_land.at[h], z_ss.at[h], z_rs.at[h], chip_at(y, 1 - zl))

        def to_z(q):
            h = q // 2

            @pl.when(core == q % 2)
            def _():
                out_wait(h).wait()

                def total(zi):
                    value = acc[q, tok_place(y, zi), feats]
                    for d in range(ranks_y - 1):
                        at = pl.ds(aligned((d * 2 + zi) * part, part), part)
                        value = value + out_land[h, at].astype(F32)
                    return value

                z_send[h] = total(1 - zl).astype(BF16)
                z_copy(h).start()
                acc[q, place, feats] = total(zl)

        def finish(q):
            h = q // 2

            @pl.when(core == q % 2)
            def _():
                total = acc[q, place, feats]
                if q == CHUNKS - 1:
                    out_wait(h).wait()
                    for d in range((ranks_y - 1) * 2):
                        total = total + out_land[h, pl.ds(d * part, part)].astype(F32)
                z_copy(h).wait()
                out[pl.ds(h * part, part), :] = total + z_land[h].astype(F32)
                pair_copy(q).wait_send()

            @pl.when(core != q % 2)
            def _():
                core_copy(h).wait_send()

        def scope(name, function, *given):
            with jax.named_scope(name):
                function(*given)

        scope("tokens_out", tokens_out, 0)
        acc[...] = jnp.zeros_like(acc)
        scope("prepare", prepare)
        if OUT_AT[0] < 0:
            scope("tokens_out", tokens_out, 1)
        scope("tokens_pair", tokens_pair, 0)
        if RELAY_AT[0] < 0:
            scope("tokens_relay", tokens_relay, 1)
        scope("low_rank", low_rank, 0)

        events = {}
        for q in range(1, CHUNKS):
            if OUT_AT[q - 1] >= 0:
                events.setdefault(OUT_AT[q - 1], []).append(("tokens_out", tokens_out, q))
            if RELAY_AT[q - 1] >= 0:
                events.setdefault(RELAY_AT[q - 1], []).append(("tokens_relay", tokens_relay, q))
            events.setdefault(PAIR_AT[q - 1], []).append(("tokens_pair", tokens_pair, q))
            events.setdefault(UNITS * q - 1, []).append(("low_rank", low_rank, q))
        for q in range(CHUNKS - 1):
            done = UNITS * (q + 1) - 1 + SKEW[3]
            events.setdefault(done, []).append(("to_owning_core", to_owning_core, q))
            events.setdefault(done + AFTER[0], []).append(("to_owners", to_owners, q))
            events.setdefault(done + AFTER[1], []).append(("to_z", to_z, q))
        stages = [("first", 0, first), ("sum_1", SKEW[0], sum_1), ("sum_2", SKEW[1], sum_2)]
        stages += [("relay", SKEW[2], relay), ("second", SKEW[3], second)]
        steps = units + SKEW[3]
        late = [item for at, todo in sorted(events.items()) if at >= steps for item in todo]

        @pl.loop(0, (steps + UNITS - 1) // UNITS)
        def _(turn):
            for step in range(UNITS):
                for name, skew, stage in stages:
                    back, g = divmod(step - skew, UNITS)

                    @pl.when((turn + back >= 0) & (turn + back < CHUNKS))
                    def _():
                        scope(name, run, stage, turn + back, g)

                for at, todo in sorted(events.items()):
                    if at % UNITS != step or at >= steps:
                        continue

                    @pl.when(turn == at // UNITS)
                    def _():
                        for name, function, q in todo:
                            scope(name, function, q)

        last = CHUNKS - 1
        scope("to_owning_core", to_owning_core, last)
        for name, function, q in late:
            if q % 2 != last % 2:
                scope(name, function, q)
        scope("to_owners", to_owners, last)
        for name, function, q in late:
            if q % 2 == last % 2:
                scope(name, function, q)
        for q in range(CHUNKS):
            scope("finish", finish, q)

    vmem = pltpu.VMEM
    dma = pltpu.SemaphoreType.DMA
    scratch = [
        vmem((CHUNKS, rows, wide_k), BF16),
        vmem((UNITS - 1, wide_k, 2 * block), BF16),
        vmem((wide_k, block), BF16),
        vmem((columns, depth + LANE), BF16),
        vmem((units, rows, 2 * block), BF16),
        vmem((units, (ranks_x - 1) * 2 * own, 2 * block), BF16),
        vmem((units, (ranks_x - 1) * own, 2 * block), BF16),
        vmem((units, ranks_x * own, 2 * block), BF16),
        vmem((units, own, 2 * block), F32),
        vmem((units, rows, block), BF16),
        vmem((CHUNKS, rows, depth + LANE), F32),
        vmem((HALVES, rows, depth), BF16),
        vmem((HALVES, rows, depth), BF16),
        vmem((HALVES, rows, depth), BF16),
        vmem((HALVES, (ranks_y - 1) * 2 * part, depth), BF16),
        vmem((HALVES, part, depth), BF16),
        vmem((HALVES, part, depth), BF16),
        vmem((2, groups, columns), F32),
        vmem((blocks, depth), F32),
        vmem((2, depth, LANE), F32),
        vmem((2, LANE, columns), F32),
        vmem((columns, LANE), F32),
        vmem((LANE, depth), F32),
        vmem((depth, 2 * LANE), BF16),
        vmem((LANE, depth), BF16),
        dma((UNITS,)),
        dma((1,)),
        dma((9,)),
        dma((HALVES,)), dma((chips - 1,)), dma((HALVES,)), dma((HALVES,)), dma((CHUNKS,)), dma((CHUNKS,)),
        dma((units,)),
        dma((WINDOW,)), dma((WINDOW,)), dma((WINDOW,)), dma((units,)),
        dma((HALVES,)), dma((HALVES,)), dma((HALVES,)), dma((HALVES,)),
        dma((HALVES,)), dma((HALVES,)),
    ]
    return kernel, scratch


def solution(mesh):
    n_wide, n_narrow = mesh.shape["wide"], mesh.shape["narrow"]

    def shards(tokens, gate_codes, up_codes, *rest):
        tok_rows = tokens.shape[0]
        depth, columns = gate_codes.shape
        kernel, scratch = make_kernel(n_wide, n_narrow, depth, columns, tok_rows)
        in_specs = [pl.BlockSpec(memory_space=pltpu.VMEM)] + [
            pl.BlockSpec(memory_space=pl.ANY)
        ] * 12
        return pl.pallas_call(
            kernel,
            out_shape=jax.ShapeDtypeStruct((tok_rows, depth), F32),
            in_specs=in_specs,
            out_specs=pl.BlockSpec(memory_space=pltpu.VMEM),
            scratch_shapes=scratch,
            compiler_params=pltpu.CompilerParams(
                collective_id=0, has_side_effects=True, vmem_limit_bytes=60 << 20
            ),
        )(tokens, gate_codes, up_codes, *rest)

    placed = (
        P("wide", "narrow"),
        P("narrow", "wide"),
        P("narrow", "wide"),
        P("narrow", "wide"),
        P("narrow", "wide"),
        P("wide", "narrow"),
        P("wide", "narrow"),
        P("narrow", None),
        P(None, "wide"),
        P("narrow", None),
        P(None, "wide"),
        P("wide", None),
        P(None, "narrow"),
    )
    return jax.shard_map(
        shards, mesh=mesh, in_specs=placed, out_specs=P("wide", "narrow"), check_vma=False
    )
```

```python
import jax
import jax.numpy as jnp
from jax import lax
from jax.experimental import pallas as pl
from jax.experimental.pallas import tpu as pltpu
from jax.sharding import PartitionSpec as P

MESH = pl.DeviceIdType.MESH
F32 = jnp.float32
BF16 = jnp.bfloat16
LANE = 128
HALVES = 2
CHUNKS = 4
UNITS = 7
X_FIRST = (1, 3, 5)
SKEW = (4, 8, 12, 16)
AFTER = (3, 9)
OUT_AT = (-1, 0, 3)
RELAY_AT = (-1, 4, 10)
PAIR_AT = (3, 9, 16)
FAR_FIRST = (2, 1, 3)
WINDOW = 14
SPREAD = 3


def remote(src, dst, send_sem, recv_sem, device):
    return pltpu.make_async_remote_copy(
        src_ref=src,
        dst_ref=dst,
        send_sem=send_sem,
        recv_sem=recv_sem,
        device_id=device,
        device_id_type=MESH,
    )


def aligned(value, size):
    return pl.multiple_of(value, size)


def make_kernel(n_wide, n_narrow, depth, columns, tok_rows):
    chips = n_wide // 2
    ranks_y = chips // 2
    part = tok_rows // HALVES
    rows = chips * part
    ranks_x = n_narrow // 2
    own = rows // n_narrow
    groups = depth // LANE
    blocks = columns // LANE
    wide_k = depth + 2 * LANE
    block = 2 * LANE
    units = CHUNKS * UNITS
    last_block = (UNITS - 1) * block

    def kernel(
        tok, gate_codes, up_codes, gate_scale, up_scale, down_codes, down_scale,
        gate_left, gate_right, up_left, up_right, down_left, down_right,
        out,
        x_all, w_up, w_last, w_down, partial, land_1, land_2, half_sum, own_sum, hidden, acc,
        core_send, core_land, out_send, out_land, z_send, z_land,
        scale_v, dscale_v, left_v, right_v, dleft_v, dright_v, left_b, dright_b,
        load_w, load_d, load_s,
        tok_send, tok_first, tok_recv, tok_recv_z, pair_send, pair_recv,
        unit_send, rs_1, rs_2, hid_recv_1, hid_recv_2,
        core_ss, core_rs, out_ss, out_rs, z_ss, z_rs,
    ):
        w = lax.axis_index("wide")
        n = lax.axis_index("narrow")
        core, y, zl = lax.rem(w, 2), lax.rem(w // 2, ranks_y), w // chips
        x, zh = n // 2, lax.rem(n, 2)
        sibling = (w + 1 - 2 * core, n)
        z_peer = (w, x * 2 + (1 - zh))

        def y_peer(d):
            return lax.rem(y + d, ranks_y)

        def chip_at(yi, zi):
            return (zi * chips + yi * 2 + core, n)

        def tok_place(yi, zi, count=1):
            return pl.ds(aligned((yi * 2 + zi) * part, part), count * part)

        def x_peer(d):
            return lax.rem(x + d, ranks_x)

        small = [
            pltpu.make_async_copy(gate_left, left_v.at[0], load_s.at[0]),
            pltpu.make_async_copy(up_left, left_v.at[1], load_s.at[1]),
            pltpu.make_async_copy(gate_scale, scale_v.at[0], load_s.at[2]),
            pltpu.make_async_copy(up_scale, scale_v.at[1], load_s.at[3]),
            pltpu.make_async_copy(gate_right, right_v.at[0], load_s.at[4]),
            pltpu.make_async_copy(up_right, right_v.at[1], load_s.at[5]),
            pltpu.make_async_copy(down_scale, dscale_v, load_s.at[6]),
            pltpu.make_async_copy(down_left, dleft_v, load_s.at[7]),
            pltpu.make_async_copy(down_right, dright_v, load_s.at[8]),
        ]
        feats = pl.ds(0, depth)

        def cols_of(g, size=block):
            return pl.ds(aligned(g * block, size), size)

        def up_loads(g, target, size):
            return [
                pltpu.make_async_copy(
                    codes.at[:, cols_of(g, size)],
                    target.at[feats, pl.ds(i * size, size)],
                    load_w.at[g],
                )
                for i, codes in enumerate((gate_codes, up_codes))
            ]

        def down_load(g):
            here = pl.ds(aligned(g * LANE, LANE), LANE)
            return pltpu.make_async_copy(
                down_codes.at[here, :], w_down.at[here, feats], load_d.at[0]
            )

        with jax.named_scope("issue"):
            for copy in small[:6]:
                copy.start()

            @pl.loop(0, UNITS - 1)
            def _(g):
                for copy in up_loads(g, w_up.at[g], block):
                    copy.start()

            for copy in up_loads(UNITS - 1, w_last, LANE) + small[6:]:
                copy.start()

            @pl.loop(0, blocks)
            def _(g):
                down_load(g).start()

        with jax.named_scope("greet"):
            barrier = pltpu.get_barrier_semaphore()
            greet = [chip_at(y_peer(d), zi) for d in range(1, ranks_y) for zi in range(2)]
            greet += [chip_at(y, 1 - zl)]
            greet += [(w, x_peer(d) * 2 + zi) for d in range(1, ranks_x) for zi in range(2)]
            greet += [z_peer, sibling]
            for device in greet:
                pl.semaphore_signal(barrier, inc=1, device_id=device, device_id_type=MESH)
            pl.semaphore_wait(barrier, len(greet))

        place = tok_place(y, zl)

        def tokens_out(q):
            h, c = q // 2, q % 2

            @pl.when(core == c)
            def _():
                def send(recv, device):
                    remote(
                        tok.at[pl.ds(h * part, part), :],
                        x_all.at[q, place, feats],
                        tok_send.at[h],
                        recv,
                        device,
                    ).start()

                send(tok_first.at[0] if q == 0 else tok_recv_z.at[h], chip_at(y, 1 - zl))
                for d in range(1, ranks_y):
                    send(tok_first.at[d] if q == 0 else tok_recv.at[h], chip_at(y_peer(d), zl))
                    if q == 0:
                        send(tok_first.at[ranks_y - 1 + d], chip_at(y_peer(d), 1 - zl))
                x_all[q, place, feats] = tok[pl.ds(h * part, part), :]

        def tokens_got(q, count, recv):
            got = x_all.at[q, pl.ds(0, count * part), feats]
            return remote(got, got, tok_send.at[q // 2], recv.at[q // 2], sibling)

        def tokens_relay(q):
            @pl.when(core == q % 2)
            def _():
                tokens_got(q, 1, tok_recv_z).wait_recv()
                here = x_all.at[q, tok_place(y, 1 - zl), feats]
                for d in range(1, ranks_y):
                    remote(
                        here, here, tok_send.at[q // 2], tok_recv.at[q // 2], chip_at(y_peer(d), zl)
                    ).start()

        def pair_copy(q):
            both = x_all.at[q, :, feats]
            return remote(both, both, pair_send.at[q], pair_recv.at[q], sibling)

        def pass_on(at):
            here = x_all.at[0, at, feats]
            remote(here, here, pair_send.at[0], pair_recv.at[0], sibling).start()

        def tokens_pair(q):
            @pl.when(core == q % 2)
            def _():
                if q > 0:
                    tokens_got(q, chips - 2, tok_recv).wait_recv()
                    pair_copy(q).start()
                else:
                    pass_on(place)
                    for d in (0, 1, 3, 4, 6, 2, 5):
                        side = 0 if d == 0 else (d - 1) % (ranks_y - 1) + 1
                        yi = lax.rem(y + ranks_y - side, ranks_y)
                        here = tok_place(yi, zl if 0 < d < ranks_y else 1 - zl)
                        got = x_all.at[q, here, feats]
                        remote(got, got, tok_send.at[0], tok_first.at[d], sibling).wait_recv()
                        pass_on(here)
                tokens_got(q, chips - 1, tok_recv).wait_send()

        def low_rank(q):
            @pl.when(core != q % 2)
            def _():
                pair_copy(q).wait_recv()

            x_all[q, :, pl.ds(depth, 2 * LANE)] = jnp.dot(
                x_all[q, :, feats], left_b[...], preferred_element_type=F32
            ).astype(BF16)

        def prepare():
            for copy in small[:6]:
                copy.wait()
            left_b[:, pl.ds(0, LANE)] = left_v[0].astype(BF16)
            left_b[:, pl.ds(LANE, LANE)] = left_v[1].astype(BF16)

            def widen(g, target, size):
                whole = target.at[feats, :]
                pltpu.make_async_copy(whole, whole, load_w.at[g]).wait()
                for i in range(2):
                    here = pl.ds(i * size, size)
                    for k in range(groups):
                        at = pl.ds(k * LANE, LANE)
                        scale = scale_v[i, pl.ds(k, 1), cols_of(g, size)]
                        target[at, here] = (target[at, here].astype(F32) * scale).astype(BF16)
                    right = right_v[i, :, cols_of(g, size)].astype(BF16)
                    target[pl.ds(depth + i * LANE, LANE), here] = right
                    target[pl.ds(depth + (1 - i) * LANE, LANE), here] = jnp.zeros_like(right)

            @pl.loop(0, UNITS - 1)
            def _(g):
                widen(g, w_up.at[g], block)

            widen(UNITS - 1, w_last, LANE)
            for copy in small[6:]:
                copy.wait()
            dright_b[...] = dright_v[...].astype(BF16)
            whole = w_down.at[:, feats]
            pltpu.make_async_copy(whole, whole, load_d.at[0]).wait()

            @pl.loop(0, blocks)
            def _(g):
                here = pl.ds(aligned(g * LANE, LANE), LANE)
                scale = dscale_v[pl.ds(g, 1), :]
                w_down[here, feats] = (w_down[here, feats].astype(F32) * scale).astype(BF16)
                w_down[here, pl.ds(depth, LANE)] = dleft_v[here, :].astype(BF16)

        def run(stage, q, g):
            stage(q * UNITS + g, q, g, g in X_FIRST, LANE if g == UNITS - 1 else block)

        def start_of(x_first, xi, zi):
            return aligned(xi * 2 * own + zi * own if x_first else zi * ranks_x * own + xi * own, own)

        def slot(u):
            return u - jnp.where(u >= WINDOW, WINDOW, 0)

        def arrival(recv, u):
            return recv.at[u if recv is hid_recv_2 else slot(u)]

        def bytes_of(buffer, u, count, size, recv):
            at = buffer.at[u, pl.ds(0, count), pl.ds(0, size)]
            return remote(at, at, unit_send.at[u], arrival(recv, u), sibling)

        def wait_1(u, x_first, size):
            count = (ranks_x - 1) * 2 * own if x_first else ranks_x * own
            return bytes_of(land_1, u, count, size, rs_1)

        def wait_2(u, x_first, size):
            count = own if x_first else (ranks_x - 1) * own
            return bytes_of(land_2, u, count, size, rs_2)

        def first(u, q, g, x_first, size):
            cols = pl.ds(0, 2 * size)
            weights = w_up[g] if size == block else w_last[...]
            partial[u, :, cols] = jnp.dot(
                x_all[q], weights, preferred_element_type=F32
            ).astype(BF16)
            if x_first:
                for d in FAR_FIRST:
                    xi = x_peer(d)
                    remote(
                        partial.at[u, pl.ds(start_of(True, xi, 0), 2 * own), cols],
                        land_1.at[u, pl.ds((d - 1) * 2 * own, 2 * own), cols],
                        unit_send.at[u],
                        rs_1.at[slot(u)],
                        (w, xi * 2 + zh),
                    ).start()
            else:
                remote(
                    partial.at[u, pl.ds(start_of(False, 0, 1 - zh), ranks_x * own), cols],
                    land_1.at[u, pl.ds(0, ranks_x * own), cols],
                    unit_send.at[u],
                    rs_1.at[slot(u)],
                    z_peer,
                ).start()

        def hidden_copy(u, at, size, recv, device):
            here = hidden.at[u, at, pl.ds(0, size)]
            return remote(here, here, unit_send.at[u], arrival(recv, u), device)

        def activate(u, q, total, x_first, size):
            gate, up = total[:, :size], total[:, size:]
            mine = pl.ds(start_of(x_first, x, zh), own)
            hidden[u, mine, pl.ds(0, size)] = (gate / (1.0 + jnp.exp(-gate)) * up).astype(BF16)
            along_z = hid_recv_1 if x_first else hid_recv_2
            along_x = hid_recv_2 if x_first else hid_recv_1
            hidden_copy(u, mine, size, along_z, z_peer).start()
            for d in FAR_FIRST:
                xi = x_peer(d) * 2
                hidden_copy(u, mine, size, along_x, (w, xi + zh)).start()

            @pl.when(q >= SPREAD)
            def _():
                for d in FAR_FIRST:
                    device = (w, x_peer(d) * 2 + 1 - zh)
                    hidden_copy(u, mine, size, hid_recv_2, device).start()

        def sum_1(u, q, g, x_first, size):
            cols = pl.ds(0, 2 * size)
            wait_1(u, x_first, 2 * size).wait_recv()
            if x_first:

                def total(zi):
                    value = partial[u, pl.ds(start_of(True, x, zi), own), cols].astype(F32)
                    for d in range(ranks_x - 1):
                        at = pl.ds(aligned(d * 2 * own + zi * own, own), own)
                        value = value + land_1[u, at, cols].astype(F32)
                    return value

                half_sum[u, pl.ds(0, own), cols] = total(1 - zh).astype(BF16)
                remote(
                    half_sum.at[u, pl.ds(0, own), cols],
                    land_2.at[u, pl.ds(0, own), cols],
                    unit_send.at[u],
                    rs_2.at[slot(u)],
                    z_peer,
                ).start()
                own_sum[u, :, cols] = total(zh)
            else:
                group = pl.ds(start_of(False, 0, zh), ranks_x * own)
                got = pl.ds(0, ranks_x * own)
                half_sum[u, got, cols] = (
                    partial[u, group, cols].astype(F32) + land_1[u, got, cols].astype(F32)
                ).astype(BF16)
                for d in FAR_FIRST:
                    xi = x_peer(d)
                    remote(
                        half_sum.at[u, pl.ds(aligned(xi * own, own), own), cols],
                        land_2.at[u, pl.ds((d - 1) * own, own), cols],
                        unit_send.at[u],
                        rs_2.at[slot(u)],
                        (w, xi * 2 + zh),
                    ).start()
                mine = pl.ds(aligned(x * own, own), own)
                own_sum[u, :, cols] = (
                    partial[u, pl.ds(start_of(False, x, zh), own), cols].astype(F32)
                    + land_1[u, mine, cols].astype(F32)
                )

        def sum_2(u, q, g, x_first, size):
            wait_2(u, x_first, 2 * size).wait_recv()
            total = own_sum[u, :, pl.ds(0, 2 * size)]
            for d in range(1 if x_first else ranks_x - 1):
                total = total + land_2[u, pl.ds(d * own, own), pl.ds(0, 2 * size)].astype(F32)
            activate(u, q, total, x_first, size)

        def wait_early(u, x_first, size):
            count = own if x_first else (ranks_x - 1) * own
            return bytes_of(hidden, u, count, size, hid_recv_1)

        def wait_late(u, x_first, size):
            count = (ranks_x - 1) * 2 * own if x_first else ranks_x * own
            return bytes_of(hidden, u, count, size, hid_recv_2)

        def relay(u, q, g, x_first, size):
            wait_early(u, x_first, size).wait_recv()

            @pl.when(q < SPREAD)
            def _():
                for d in FAR_FIRST:
                    xi = x_peer(d)
                    if x_first:
                        at = pl.ds(start_of(True, x, 1 - zh), own)
                        device = (w, xi * 2 + zh)
                    else:
                        at = pl.ds(start_of(False, xi, zh), own)
                        device = z_peer
                    hidden_copy(u, at, size, hid_recv_2, device).start()

        def second(u, q, g, x_first, size):
            wait_late(u, x_first, size).wait_recv()
            acc[q] += jnp.dot(
                hidden[u, :, pl.ds(0, size)],
                w_down[cols_of(g, size), :],
                preferred_element_type=F32,
            )
            sent = w_down.at[pl.ds(0, (n_narrow - 1) * own * 3), pl.ds(0, size)]
            remote(sent, sent, unit_send.at[u], hid_recv_2.at[u], sibling).wait_send()

        def core_copy(h):
            return remote(core_send.at[h], core_land.at[h], core_ss.at[h], core_rs.at[h], sibling)

        def to_owning_core(q):
            low = acc[q, :, pl.ds(depth, LANE)].astype(BF16)
            acc[q, :, feats] += jnp.dot(low, dright_b[...], preferred_element_type=F32)

            @pl.when(core != q % 2)
            def _():
                core_send[q // 2] = acc[q, :, feats].astype(BF16)
                core_copy(q // 2).start()

        def out_copy(h, src, dst, send, recv, device):
            return remote(src, dst, send.at[h], recv.at[h], device)

        def to_owners(q):
            h = q // 2

            @pl.when(core == q % 2)
            def _():
                core_copy(h).wait_recv()
                both = acc[q, :, feats] + core_land[h].astype(F32)
                acc[q, :, feats] = both
                out_send[h] = both.astype(BF16)
                for d in range(1, ranks_y):
                    yi = y_peer(d)
                    if q < CHUNKS - 1:
                        at = pl.ds((d - 1) * 2 * part, 2 * part)
                        remote(
                            out_send.at[h, tok_place(yi, 0, 2)],
                            out_land.at[h, at],
                            out_ss.at[h],
                            out_rs.at[h],
                            chip_at(yi, zl),
                        ).start()
                        continue
                    for zi in range(2):
                        at = pl.ds(aligned(((d - 1) * 2 + zl) * part, part), part)
                        remote(
                            out_send.at[h, tok_place(yi, zi)],
                            out_land.at[h, at],
                            out_ss.at[h],
                            out_rs.at[h],
                            chip_at(yi, zi),
                        ).start()
                if q == CHUNKS - 1:
                    remote(
                        out_send.at[h, tok_place(y, 1 - zl)],
                        z_land.at[h],
                        z_ss.at[h],
                        z_rs.at[h],
                        chip_at(y, 1 - zl),
                    ).start()

        def out_wait(h):
            got = out_land.at[h]
            return remote(got, got, out_ss.at[h], out_rs.at[h], sibling)

        def z_copy(h):
            return remote(z_send.at[h], z_land.at[h], z_ss.at[h], z_rs.at[h], chip_at(y, 1 - zl))

        def to_z(q):
            h = q // 2

            @pl.when(core == q % 2)
            def _():
                out_wait(h).wait()

                def total(zi):
                    value = acc[q, tok_place(y, zi), feats]
                    for d in range(ranks_y - 1):
                        at = pl.ds(aligned((d * 2 + zi) * part, part), part)
                        value = value + out_land[h, at].astype(F32)
                    return value

                z_send[h] = total(1 - zl).astype(BF16)
                z_copy(h).start()
                acc[q, place, feats] = total(zl)

        def finish(q):
            h = q // 2

            @pl.when(core == q % 2)
            def _():
                total = acc[q, place, feats]
                if q == CHUNKS - 1:
                    out_wait(h).wait()
                    for d in range((ranks_y - 1) * 2):
                        total = total + out_land[h, pl.ds(d * part, part)].astype(F32)
                z_copy(h).wait()
                out[pl.ds(h * part, part), :] = total + z_land[h].astype(F32)
                pair_copy(q).wait_send()

            @pl.when(core != q % 2)
            def _():
                core_copy(h).wait_send()

        def scope(name, function, *given):
            with jax.named_scope(name):
                function(*given)

        scope("tokens_out", tokens_out, 0)
        acc[...] = jnp.zeros_like(acc)
        scope("prepare", prepare)
        if OUT_AT[0] < 0:
            scope("tokens_out", tokens_out, 1)
        scope("tokens_pair", tokens_pair, 0)
        if RELAY_AT[0] < 0:
            scope("tokens_relay", tokens_relay, 1)
        scope("low_rank", low_rank, 0)

        events = {}
        for q in range(1, CHUNKS):
            if OUT_AT[q - 1] >= 0:
                events.setdefault(OUT_AT[q - 1], []).append(("tokens_out", tokens_out, q))
            if RELAY_AT[q - 1] >= 0:
                events.setdefault(RELAY_AT[q - 1], []).append(("tokens_relay", tokens_relay, q))
            events.setdefault(PAIR_AT[q - 1], []).append(("tokens_pair", tokens_pair, q))
            events.setdefault(UNITS * q - 1, []).append(("low_rank", low_rank, q))
        for q in range(CHUNKS - 1):
            done = UNITS * (q + 1) - 1 + SKEW[3]
            events.setdefault(done, []).append(("to_owning_core", to_owning_core, q))
            events.setdefault(done + AFTER[0], []).append(("to_owners", to_owners, q))
            events.setdefault(done + AFTER[1], []).append(("to_z", to_z, q))
        stages = [("first", 0, first), ("sum_1", SKEW[0], sum_1), ("sum_2", SKEW[1], sum_2)]
        stages += [("relay", SKEW[2], relay), ("second", SKEW[3], second)]
        steps = units + SKEW[3]
        late = [item for at, todo in sorted(events.items()) if at >= steps for item in todo]

        @pl.loop(0, (steps + UNITS - 1) // UNITS)
        def _(turn):
            for step in range(UNITS):
                for name, skew, stage in stages:
                    back, g = divmod(step - skew, UNITS)

                    @pl.when((turn + back >= 0) & (turn + back < CHUNKS))
                    def _():
                        scope(name, run, stage, turn + back, g)

                for at, todo in sorted(events.items()):
                    if at % UNITS != step or at >= steps:
                        continue

                    @pl.when(turn == at // UNITS)
                    def _():
                        for name, function, q in todo:
                            scope(name, function, q)

        last = CHUNKS - 1
        scope("to_owning_core", to_owning_core, last)
        for name, function, q in late:
            if q % 2 != last % 2:
                scope(name, function, q)
        scope("to_owners", to_owners, last)
        for name, function, q in late:
            if q % 2 == last % 2:
                scope(name, function, q)
        for q in range(CHUNKS):
            scope("finish", finish, q)

    vmem = pltpu.VMEM
    dma = pltpu.SemaphoreType.DMA
    scratch = [
        vmem((CHUNKS, rows, wide_k), BF16),
        vmem((UNITS - 1, wide_k, 2 * block), BF16),
        vmem((wide_k, block), BF16),
        vmem((columns, depth + LANE), BF16),
        vmem((units, rows, 2 * block), BF16),
        vmem((units, (ranks_x - 1) * 2 * own, 2 * block), BF16),
        vmem((units, (ranks_x - 1) * own, 2 * block), BF16),
        vmem((units, ranks_x * own, 2 * block), BF16),
        vmem((units, own, 2 * block), F32),
        vmem((units, rows, block), BF16),
        vmem((CHUNKS, rows, depth + LANE), F32),
        vmem((HALVES, rows, depth), BF16),
        vmem((HALVES, rows, depth), BF16),
        vmem((HALVES, rows, depth), BF16),
        vmem((HALVES, (ranks_y - 1) * 2 * part, depth), BF16),
        vmem((HALVES, part, depth), BF16),
        vmem((HALVES, part, depth), BF16),
        vmem((2, groups, columns), F32),
        vmem((blocks, depth), F32),
        vmem((2, depth, LANE), F32),
        vmem((2, LANE, columns), F32),
        vmem((columns, LANE), F32),
        vmem((LANE, depth), F32),
        vmem((depth, 2 * LANE), BF16),
        vmem((LANE, depth), BF16),
        dma((UNITS,)),
        dma((1,)),
        dma((9,)),
        dma((HALVES,)), dma((chips - 1,)), dma((HALVES,)), dma((HALVES,)), dma((CHUNKS,)), dma((CHUNKS,)),
        dma((units,)),
        dma((WINDOW,)), dma((WINDOW,)), dma((WINDOW,)), dma((units,)),
        dma((HALVES,)), dma((HALVES,)), dma((HALVES,)), dma((HALVES,)),
        dma((HALVES,)), dma((HALVES,)),
    ]
    return kernel, scratch


def solution(mesh):
    n_wide, n_narrow = mesh.shape["wide"], mesh.shape["narrow"]

    def shards(tokens, gate_codes, up_codes, *rest):
        tok_rows = tokens.shape[0]
        depth, columns = gate_codes.shape
        kernel, scratch = make_kernel(n_wide, n_narrow, depth, columns, tok_rows)
        in_specs = [pl.BlockSpec(memory_space=pltpu.VMEM)] + [
            pl.BlockSpec(memory_space=pl.ANY)
        ] * 12
        return pl.pallas_call(
            kernel,
            out_shape=jax.ShapeDtypeStruct((tok_rows, depth), F32),
            in_specs=in_specs,
            out_specs=pl.BlockSpec(memory_space=pltpu.VMEM),
            scratch_shapes=scratch,
            compiler_params=pltpu.CompilerParams(
                collective_id=0, has_side_effects=True, vmem_limit_bytes=60 << 20
            ),
        )(tokens, gate_codes, up_codes, *rest)

    placed = (
        P("wide", "narrow"),
        P("narrow", "wide"),
        P("narrow", "wide"),
        P("narrow", "wide"),
        P("narrow", "wide"),
        P("wide", "narrow"),
        P("wide", "narrow"),
        P("narrow", None),
        P(None, "wide"),
        P("narrow", None),
        P(None, "wide"),
        P("wide", None),
        P(None, "narrow"),
    )
    return jax.shard_map(
        shards, mesh=mesh, in_specs=placed, out_specs=P("wide", "narrow"), check_vma=False
    )
```
